1024 devices in a mesh: dp: 128 (over z_hi, x, y, core), mp: 8 (over z_lo).
Axes of the slice: x: 4, y: 8, z: 16 (z_hi: 2, z_lo: 8; z = z_hi * 8 + z_lo), core: 2. Of those that a mesh axis runs over, the one named last changes fastest.
Arguments:
- tokens: bfloat16 [32768, 4096], P('dp'), may hold values from -72 to 72
- qkv_weight: bfloat16 [4096, 3, 2048], P('dp', None, 'mp'), may hold values from -0.09375 to 0.09375
- out_weight: bfloat16 [2048, 4096], P('mp'), may hold values from -0.125 to 0.125
Outputs:
- attended: bfloat16 [32768, 4096], P(('dp', 'mp'))
The draws below stay inside these ranges and needn't reach their ends.
All inputs are finite; a program needn't handle non-finite values.
Results may differ from the reference program's by a relative error of at most 0.022.
The reference program's roundings to bfloat16 on the way (of `projected`, `attn_weights`, `mixed` and `terms`) count: a program that leaves them out, or rounds other values in their place, can miss the bound.
Values may be sent and summed in bfloat16 or wider, within the bound.
No kernel may reach another device: no remote copies, remote signals or barrier semaphores. Data moves between devices by JAX's collectives and lax.ppermute only.
A program may use at most 32 MiB of HBM per device.

```python
import math
import jax
import jax.numpy as jnp
from jax import lax

D = 4096
HD = 128
HEAD_DEV = 2
HEADS = 16
TOK = 256
TOKENS = 32768
N_DP = 128
N_MP = 8


def draw_tokens(key, part):
    key = jax.random.fold_in(key, 11)
    first, second = jax.random.split(key, 2)
    base = jnp.clip(jax.random.normal(first, (TOKENS, D), jnp.float32), -6.0, 6.0)
    spread = jnp.exp(jax.random.uniform(second, (TOKENS, 1), jnp.float32, math.log(0.5), math.log(2.0)))
    return (base * spread).astype(jnp.bfloat16)


def steps_of(own_key, dims, pieces, least, high):
    loudness, own = 1.0, jax.random.fold_in(own_key, 6)
    for axis_at, parts in pieces:
        steps = jnp.exp(jax.random.uniform(jax.random.fold_in(own, axis_at), (parts,), jnp.float32, least / len(pieces), high / len(pieces)))
        loudness = loudness * jnp.repeat(steps, dims[axis_at] // parts).reshape([-1 if axis == axis_at else 1 for axis in range(len(dims))])
    return loudness


def normal_values(stream_key, shape, scale, limit, cuts=(), held_as=jnp.bfloat16):
    array = scale * jax.random.normal(stream_key, shape, jnp.float32)
    if cuts:
        array = array * steps_of(stream_key, shape, cuts, -0.22, 0.18)
    return jnp.clip(array, -limit, limit).astype(held_as)


def setup_inputs(seed: int = 0) -> dict:
    arg_keys = jax.random.split(jax.random.key(seed), 4)
    return {
        "tokens": draw_tokens(jax.random.fold_in(arg_keys[3], 71), 0),
        "qkv_weight": normal_values(arg_keys[1], (D, 3, HEADS * HD), D ** -0.5, 0.09375, ((0, 128), (2, 8))),
        "out_weight": normal_values(arg_keys[2], (HEADS * HD, D), (HEADS * HD) ** -0.5, 0.125, ((0, 8),)),
    }


def attend(queries, key_rows, values):
    scores = jnp.einsum('qhe,khe->hqk', queries.astype(jnp.float32), key_rows.astype(jnp.float32), precision=lax.Precision.HIGHEST) / math.sqrt(queries.shape[2])
    attn_weights = jax.nn.softmax(scores, axis=-1).astype(jnp.bfloat16)
    mixed = jnp.einsum('hqk,khe->qhe', attn_weights.astype(jnp.float32), values.astype(jnp.float32), precision=lax.Precision.HIGHEST)
    return mixed.astype(jnp.bfloat16)

def reference(tokens, qkv_weight, out_weight):
    weight_wide = qkv_weight.astype(jnp.float32)
    out_blocks = out_weight.astype(jnp.float32).reshape(N_MP, HEAD_DEV * HD, D)

    def one_group(group_tokens):
        projected = jnp.einsum('td,dsc->tsc', group_tokens.astype(jnp.float32), weight_wide, precision=lax.Precision.HIGHEST).astype(jnp.bfloat16)
        queries = projected[:, 0].reshape(TOK, HEADS, HD)
        key_rows = projected[:, 1].reshape(TOK, HEADS, HD)
        values = projected[:, 2].reshape(TOK, HEADS, HD)
        mixed = attend(queries, key_rows, values).reshape(TOK, N_MP, HEAD_DEV * HD)
        terms = jnp.einsum('tmc,mcd->mtd', mixed.astype(jnp.float32), out_blocks, precision=lax.Precision.HIGHEST).astype(jnp.bfloat16)
        terms = lax.optimization_barrier(terms)
        return lax.optimization_barrier(jnp.sum(terms.astype(jnp.float32), axis=0)).astype(jnp.bfloat16)
    grouped = lax.map(one_group, tokens.reshape(N_DP, TOK, D))
    return grouped.reshape(TOKENS, D)
```

```python
import functools
import math

import jax
import jax.numpy as jnp
from jax import lax
from jax.experimental import pallas as pl
from jax.experimental.pallas import tpu as pltpu
from jax.sharding import Mesh
from jax.sharding import PartitionSpec as P

HD = 128
ZH, X, YQ, YP, C = 2, 4, 4, 2, 2
RG, CB = 2, 4
AXES = ("zh", "x", "yq", "yp", "c", "rg", "cb")
DP, MP = AXES[:5], AXES[5:]


def spread(block, axes, n):
    return lax.all_to_all(jnp.broadcast_to(block[None], (n,) + block.shape), axes, 0, 0, tiled=True)


def attend_kernel(own_ref, other_ref, w_ref, out_ref):
    part = w_ref.shape[3]
    span = YQ * YP * part
    totals = [None, None]
    for zh in range(ZH):
        for x in range(X):
            weight = jnp.concatenate(
                [w_ref[x * YP + yp, yq, zh] for yq in range(YQ) for yp in range(YP)], axis=0
            )
            start = (zh * X + x) * span
            for g, ref in enumerate((own_ref, other_ref)):
                product = jnp.dot(
                    ref[:, start : start + span], weight, preferred_element_type=jnp.float32
                )
                totals[g] = product if totals[g] is None else totals[g] + product
    for g in range(2):
        projected = totals[g].astype(jnp.bfloat16)
        queries, key_rows, values = (projected[:, i * HD : (i + 1) * HD] for i in range(3))
        scores = lax.dot_general(
            queries, key_rows, (((1,), (1,)), ((), ())), preferred_element_type=jnp.float32
        ) * (1.0 / math.sqrt(HD))
        raised = jnp.exp(scores - jnp.max(scores, axis=-1, keepdims=True))
        attn = (raised / jnp.sum(raised, axis=-1, keepdims=True)).astype(jnp.bfloat16)
        out_ref[g] = jnp.dot(attn, values, preferred_element_type=jnp.float32).astype(jnp.bfloat16)


def project_kernel(mixed_ref, w_ref, out_ref):
    total = None
    for block in range(mixed_ref.shape[1]):
        mixed = jnp.concatenate([mixed_ref[c, block] for c in range(C)], axis=1)
        weight = jnp.concatenate([w_ref[i, block] for i in range(w_ref.shape[0])], axis=0)
        term = jnp.dot(mixed, weight, preferred_element_type=jnp.float32).astype(jnp.bfloat16)
        wide = term.astype(jnp.float32)
        total = wide if total is None else total + wide
    out_ref[...] = total.astype(jnp.bfloat16)


def body(tokens, qkv_weight, out_weight):
    rows, width = tokens.shape
    k_rows = qkv_weight.shape[0]
    other = lax.ppermute(tokens, "c", [(0, 1), (1, 0)])

    heads = qkv_weight.reshape(k_rows, 3, C, HD).transpose(2, 0, 1, 3).reshape(C, k_rows, 3 * HD)
    heads = jnp.broadcast_to(heads[None], (ZH,) + heads.shape).reshape(ZH * C, k_rows, 3 * HD)
    heads = lax.all_to_all(heads, ("zh", "c"), 0, 0, tiled=True)
    heads = spread(heads, "yq", YQ)
    heads = spread(heads, ("x", "yp"), X * YP)
    heads = heads.reshape(X * YP, YQ, ZH, C * k_rows, 3 * HD)

    parts = X * C
    block = out_weight.shape[0] // parts
    columns = out_weight.shape[1] // CB
    mine = lax.axis_index("x") * C + lax.axis_index("c")
    share = lax.dynamic_slice_in_dim(out_weight, mine * block, block, 0)
    share = share.reshape(block, CB, columns).transpose(1, 0, 2)
    share = jnp.broadcast_to(share[None], (RG,) + share.shape).reshape(RG * CB, block, columns)
    share = lax.all_to_all(share, MP, 0, 0, tiled=True)
    out_full = lax.all_gather(share, ("x", "c"))

    mixed = pl.pallas_call(
        attend_kernel,
        out_shape=jax.ShapeDtypeStruct((2, rows, HD), jnp.bfloat16),
        compiler_params=pltpu.CompilerParams(vmem_limit_bytes=48 << 20),
        cost_estimate=pl.CostEstimate(flops=2 * 2 * rows * width * 3 * HD, bytes_accessed=8 << 20, transcendentals=0),
        name="attend",
    )(tokens, other, heads)
    core = lax.axis_index("c")
    mixed = jnp.where(core == 0, mixed, mixed[::-1])
    mixed = mixed.reshape(C, RG, 1, rows // RG, HD)
    mixed = jnp.broadcast_to(mixed, (C, RG, CB, rows // RG, HD)).reshape(C * RG * CB, rows // RG, HD)
    mixed = lax.all_to_all(mixed, ("c",) + MP, 0, 0, tiled=True).reshape(C, RG * CB, rows // RG, HD)

    summed = pl.pallas_call(
        project_kernel,
        out_shape=jax.ShapeDtypeStruct((rows // RG, columns), jnp.bfloat16),
        compiler_params=pltpu.CompilerParams(vmem_limit_bytes=48 << 20),
        cost_estimate=pl.CostEstimate(flops=2 * rows * 2048 * columns // RG, bytes_accessed=5 << 20, transcendentals=0),
        name="project",
    )(mixed, out_full)
    summed = summed.reshape(CB, rows // (RG * CB), columns)
    summed = lax.all_to_all(summed, "cb", 0, 0, tiled=True)
    return summed.transpose(1, 0, 2).reshape(rows // (RG * CB), CB * columns)


def solution(mesh):
    named = Mesh(mesh.devices.reshape(ZH, X, YQ, YP, C, RG, CB), AXES)
    return jax.shard_map(
        body,
        mesh=named,
        in_specs=(P(DP, None), P(DP, None, MP), P(MP, None)),
        out_specs=P(DP + MP, None),
        check_vma=False,
    )
```

```python
import math

import jax
import jax.numpy as jnp
from jax import lax
from jax.experimental import pallas as pl
from jax.experimental.pallas import tpu as pltpu
from jax.sharding import Mesh
from jax.sharding import PartitionSpec as P

HD = 128
ZH, X, Y, C = 2, 4, 8, 2
XQ, YQ = X // 2, Y // 2
RG, CB = 4, 2
AXES = ("zh", "x", "yq", "yp", "c", "rg", "cb")
DP, MP = AXES[:5], AXES[5:]


def place(zh, x, y, c):
    return ((zh * X + x % X) * Y + y % Y) * C + c


FAR = [
    [place(zh, 2 * xq + px, 2 * yq + py, c) for xq in range(XQ) for yq in range(YQ)]
    for zh in range(ZH) for c in range(C) for px in range(2) for py in range(2)
]
NEAR = [
    [place(zh, 2 * xq + (1 - 2 * c) * px, 2 * yq + (1 - 2 * c) * py, c) for px in range(2) for py in range(2)]
    for zh in range(ZH) for c in range(C) for xq in range(XQ) for yq in range(YQ)
]


ACROSS = [
    [
        (place(zh, x, y, c), place(zh ^ dz, x, y, c ^ dc))
        for zh in range(ZH) for x in range(X) for y in range(Y) for c in range(C)
    ]
    for dz, dc in ((0, 1), (1, 0), (1, 1))
]


def spread(block, groups):
    n = len(groups[0])
    blocks = jnp.broadcast_to(block[None], (n,) + block.shape)
    return lax.all_to_all(blocks, DP, 0, 0, axis_index_groups=groups, tiled=True)


def attend_kernel(own_ref, other_ref, w_ref, out_ref):
    span = Y * w_ref.shape[5]
    totals = [None, None]
    for zh in range(ZH):
        for x in range(X):
            weight = jnp.concatenate(
                [w_ref[x % 2, y % 2, x // 2, y // 2, zh] for y in range(Y)], axis=0
            )
            start = (zh * X + x) * span
            for g, ref in enumerate((own_ref, other_ref)):
                product = jnp.dot(
                    ref[:, start : start + span], weight, preferred_element_type=jnp.float32
                )
                totals[g] = product if totals[g] is None else totals[g] + product
    for g in range(2):
        projected = totals[g].astype(jnp.bfloat16)
        queries, key_rows, values = (projected[:, i * HD : (i + 1) * HD] for i in range(3))
        scores = lax.dot_general(
            queries, key_rows, (((1,), (1,)), ((), ())), preferred_element_type=jnp.float32
        ) * (1.0 / math.sqrt(HD))
        raised = jnp.exp(scores - jnp.max(scores, axis=-1, keepdims=True))
        attn = (raised / jnp.sum(raised, axis=-1, keepdims=True)).astype(jnp.bfloat16)
        out_ref[g] = jnp.dot(attn, values, preferred_element_type=jnp.float32).astype(jnp.bfloat16)


def project_kernel(mixed_ref, w_ref, out_ref, total_ref):
    block = pl.program_id(0)
    mixed = jnp.concatenate([mixed_ref[c, 0] for c in range(C)], axis=1)
    weight = jnp.concatenate([w_ref[i, 0] for i in range(w_ref.shape[0])], axis=0)
    term = jnp.dot(mixed, weight, preferred_element_type=jnp.float32).astype(jnp.bfloat16)

    @pl.when(block == 0)
    def _():
        total_ref[...] = term.astype(jnp.float32)

    @pl.when(block > 0)
    def _():
        total_ref[...] += term.astype(jnp.float32)

    @pl.when(block == pl.num_programs(0) - 1)
    def _():
        out_ref[...] = total_ref[...].astype(jnp.bfloat16)


def body(tokens, qkv_weight, out_weight):
    rows, width = tokens.shape
    k_rows = qkv_weight.shape[0]
    other = lax.ppermute(tokens, "c", [(0, 1), (1, 0)])

    heads = qkv_weight.reshape(k_rows, 3, C, HD).transpose(2, 0, 1, 3).reshape(C, k_rows, 3 * HD)
    core, half = lax.axis_index("c"), lax.axis_index("zh")
    own = jnp.where(core == 0, heads[0], heads[1])
    rest = jnp.where(core == 0, heads[1], heads[0])
    near = jnp.stack([own, lax.ppermute(rest, DP, ACROSS[0])])
    far = jnp.stack([lax.ppermute(own, DP, ACROSS[1]), lax.ppermute(rest, DP, ACROSS[2])])
    near, far = (jnp.where(core == 0, pair, pair[::-1]) for pair in (near, far))
    heads = jnp.where(half == 0, jnp.concatenate([near, far]), jnp.concatenate([far, near]))
    heads = spread(spread(heads, FAR), NEAR)
    heads = heads.reshape(2, 2, XQ, YQ, ZH, C * k_rows, 3 * HD)

    parts = X * 2 * C
    block = out_weight.shape[0] // parts
    columns = out_weight.shape[1] // CB
    mine = (lax.axis_index("x") * 2 + lax.axis_index("yp")) * C + core
    share = lax.dynamic_slice_in_dim(out_weight, mine * block, block, 0)
    share = jnp.stack([share[:, i * columns : (i + 1) * columns] for i in range(CB)])
    share = jnp.broadcast_to(share[None], (RG,) + share.shape).reshape(RG * CB, block, columns)
    share = lax.all_to_all(share, MP, 0, 0, tiled=True)
    out_full = lax.all_gather(share, ("x", "yp", "c"))

    mixed = pl.pallas_call(
        attend_kernel,
        out_shape=jax.ShapeDtypeStruct((2, rows, HD), jnp.bfloat16),
        compiler_params=pltpu.CompilerParams(vmem_limit_bytes=48 << 20),
        cost_estimate=pl.CostEstimate(flops=2 * 2 * rows * width * 3 * HD, bytes_accessed=8 << 20, transcendentals=0),
        name="attend",
    )(tokens, other, heads)
    mixed = jnp.where(core == 0, mixed, mixed[::-1])
    mixed = mixed.reshape(C, RG, 1, rows // RG, HD)
    mixed = jnp.broadcast_to(mixed, (C, RG, CB, rows // RG, HD)).reshape(C * RG * CB, rows // RG, HD)
    mixed = lax.all_to_all(mixed, ("c",) + MP, 0, 0, tiled=True).reshape(C, RG * CB, rows // RG, HD)

    summed = pl.pallas_call(
        project_kernel,
        out_shape=jax.ShapeDtypeStruct((rows // RG, columns), jnp.bfloat16),
        grid=(RG * CB,),
        in_specs=[
            pl.BlockSpec((C, 1, rows // RG, HD), lambda i: (0, i, 0, 0)),
            pl.BlockSpec((parts, 1, block, columns), lambda i: (0, i, 0, 0)),
        ],
        out_specs=pl.BlockSpec((rows // RG, columns), lambda i: (0, 0)),
        scratch_shapes=[pltpu.VMEM((rows // RG, columns), jnp.float32)],
        compiler_params=pltpu.CompilerParams(vmem_limit_bytes=48 << 20),
        cost_estimate=pl.CostEstimate(flops=2 * rows * 2048 * columns // RG, bytes_accessed=5 << 20, transcendentals=0),
        name="project",
    )(mixed, out_full)
    summed = summed.reshape(CB, rows // (RG * CB), columns)
    summed = lax.all_to_all(summed, "cb", 0, 0, tiled=True)
    return summed.transpose(1, 0, 2).reshape(rows // (RG * CB), CB * columns)


def solution(mesh):
    named = Mesh(mesh.devices.reshape(ZH, X, YQ, 2, C, RG, CB), AXES)
    return jax.shard_map(
        body,
        mesh=named,
        in_specs=(P(DP, None), P(DP, None, MP), P(MP, None)),
        out_specs=P(DP + MP, None),
        check_vma=False,
    )
```

```python
import math

import jax
import jax.numpy as jnp
from jax import lax
from jax.experimental import pallas as pl
from jax.experimental.pallas import tpu as pltpu
from jax.sharding import Mesh
from jax.sharding import PartitionSpec as P

HD = 128
ZH, X, Y, C = 2, 4, 8, 2
XQ, YQ = X // 2, Y // 2
RG, CB = 2, 4
AXES = ("zh", "x", "y", "c", "rg", "cb")
DP, MP = AXES[:4], AXES[4:]


def place(zh, x, y, c):
    return ((zh * X + x % X) * Y + y % Y) * C + c


FAR = [
    [place(zh, 2 * xq + px, 2 * yq + py, c) for xq in range(XQ) for yq in range(YQ)]
    for zh in range(ZH) for c in range(C) for px in range(2) for py in range(2)
]
NEAR = [
    [place(zh, 2 * xq + (1 - 2 * c) * px, 2 * yq + (1 - 2 * c) * py, c) for px in range(2) for py in range(2)]
    for zh in range(ZH) for c in range(C) for xq in range(XQ) for yq in range(YQ)
]


def spread(block, groups):
    n = len(groups[0])
    blocks = jnp.broadcast_to(block[None], (n,) + block.shape)
    return lax.all_to_all(blocks, DP, 0, 0, axis_index_groups=groups, tiled=True)


def attend_kernel(own_ref, other_ref, w_ref, *refs):
    out_ref = refs[-1]
    span = Y * w_ref.shape[5]
    totals = [None, None]
    for zh in range(ZH):
        for x in range(X):
            weight = jnp.concatenate(
                [w_ref[x % 2, y % 2, x // 2, y // 2, zh] for y in range(Y)], axis=0
            )
            start = (zh * X + x) * span
            for g, ref in enumerate((own_ref, other_ref)):
                product = jnp.dot(
                    ref[:, start : start + span], weight, preferred_element_type=jnp.float32
                )
                totals[g] = product if totals[g] is None else totals[g] + product
    for g in range(2):
        projected = totals[g].astype(jnp.bfloat16)
        queries, key_rows, values = (projected[:, i * HD : (i + 1) * HD] for i in range(3))
        scores = lax.dot_general(
            queries, key_rows, (((1,), (1,)), ((), ())), preferred_element_type=jnp.float32
        ) * (1.0 / math.sqrt(HD))
        raised = jnp.exp(scores - jnp.max(scores, axis=-1, keepdims=True))
        attn = (raised / jnp.sum(raised, axis=-1, keepdims=True)).astype(jnp.bfloat16)
        out_ref[g] = jnp.dot(attn, values, preferred_element_type=jnp.float32).astype(jnp.bfloat16)


def split_kernel(place_ref, w_ref, after_ref, own_ref, *out_refs):
    column, core = place_ref[0], place_ref[1]
    part, width = out_refs[0].shape
    own_ref[...] = w_ref[:, pl.ds(pl.multiple_of(column * width, width), width)]
    rows = pl.ds(pl.multiple_of(core * part, part), part)
    for i, out_ref in enumerate(out_refs):
        start = pl.multiple_of((column ^ (i + 1)) * width, width)
        out_ref[...] = w_ref[rows, pl.ds(start, width)]


def project_kernel(place_ref, mixed_ref, own_ref, held_ref, partner_ref, far_ref, near_ref):
    column, half, core = place_ref[0], place_ref[1], place_ref[2]
    rows = far_ref.shape[0]
    for out_ref, start in ((far_ref, (1 - half) * rows), (near_ref, half * rows)):
        span = pl.ds(pl.multiple_of(start, rows), rows)
        mixed = jnp.concatenate([mixed_ref[c, column, span] for c in range(C)], axis=1)
        term = jnp.dot(mixed, own_ref[...], preferred_element_type=jnp.float32).astype(jnp.bfloat16)
        total = term.astype(jnp.float32)
        for i in range(CB - 1):
            block = column ^ (i + 1)
            mixed = jnp.concatenate([mixed_ref[core, block, span], mixed_ref[1 - core, block, span]], axis=1)
            weight = jnp.concatenate([held_ref[i], partner_ref[i]], axis=0)
            term = jnp.dot(mixed, weight, preferred_element_type=jnp.float32).astype(jnp.bfloat16)
            total += term.astype(jnp.float32)
        out_ref[...] = total.astype(out_ref.dtype)


def body(tokens, qkv_weight, out_weight):
    rows, width = tokens.shape
    k_rows = qkv_weight.shape[0]
    other = lax.ppermute(tokens, "c", [(0, 1), (1, 0)])

    heads = qkv_weight.reshape(k_rows, 3, C, HD).transpose(2, 0, 1, 3).reshape(C, k_rows, 3 * HD)
    heads = jnp.broadcast_to(heads[None], (ZH,) + heads.shape).reshape(ZH * C, k_rows, 3 * HD)
    heads = lax.all_to_all(heads, ("zh", "c"), 0, 0, tiled=True)
    first = heads
    heads = spread(spread(heads, FAR), NEAR)
    heads = heads.reshape(2, 2, XQ, YQ, ZH, C * k_rows, 3 * HD)

    column, half, core = lax.axis_index("cb"), lax.axis_index("rg"), lax.axis_index("c")
    depth, columns = out_weight.shape[0], out_weight.shape[1] // CB
    smem, vmem = pl.BlockSpec(memory_space=pltpu.SMEM), pl.BlockSpec(memory_space=pltpu.VMEM)
    own_weight, *sent = pl.pallas_call(
        split_kernel,
        out_shape=[jax.ShapeDtypeStruct((depth, columns), jnp.bfloat16)]
        + [jax.ShapeDtypeStruct((depth // C, columns), jnp.bfloat16)] * (CB - 1),
        in_specs=[smem, vmem, vmem],
        out_specs=[vmem] * CB,
        compiler_params=pltpu.CompilerParams(vmem_limit_bytes=24 << 20),
        cost_estimate=pl.CostEstimate(flops=0, bytes_accessed=4 << 20, transcendentals=0),
        name="split",
    )(jnp.stack([column, core]), out_weight, first)
    held = [lax.ppermute(block, "cb", [(j, j ^ (i + 1)) for j in range(CB)]) for i, block in enumerate(sent)]

    mixed = pl.pallas_call(
        attend_kernel,
        out_shape=jax.ShapeDtypeStruct((2, rows, HD), jnp.bfloat16),
        in_specs=[vmem] * 3 + [pl.BlockSpec(memory_space=pl.ANY)] * len(held),
        compiler_params=pltpu.CompilerParams(vmem_limit_bytes=48 << 20),
        cost_estimate=pl.CostEstimate(flops=2 * 2 * rows * width * 3 * HD, bytes_accessed=8 << 20, transcendentals=0),
        name="attend",
    )(tokens, other, heads, *held)
    held = jnp.stack(held)
    partner = lax.ppermute(held, "c", [(0, 1), (1, 0)])
    mixed = jnp.where(core == 0, mixed, mixed[::-1])
    mixed = jnp.broadcast_to(mixed[:, None], (C, CB, rows, HD)).reshape(C * CB, rows, HD)
    mixed = lax.all_to_all(mixed, ("c", "cb"), 0, 0, tiled=True).reshape(C, CB, rows, HD)

    part = rows // RG
    far, near = pl.pallas_call(
        project_kernel,
        out_shape=[
            jax.ShapeDtypeStruct((part, columns), jnp.bfloat16),
            jax.ShapeDtypeStruct((part, columns), jnp.float32),
        ],
        in_specs=[smem] + [vmem] * 4,
        out_specs=[vmem] * 2,
        compiler_params=pltpu.CompilerParams(vmem_limit_bytes=24 << 20),
        cost_estimate=pl.CostEstimate(flops=2 * rows * CB * C * HD * columns, bytes_accessed=4 << 20, transcendentals=0),
        name="project",
    )(jnp.stack([column, half, core]), mixed, own_weight, held, partner)
    far = lax.ppermute(far, "rg", [(0, 1), (1, 0)])
    summed = (near + far.astype(jnp.float32)).astype(jnp.bfloat16)
    summed = summed.reshape(CB, part // CB, columns)
    summed = lax.all_to_all(summed, "cb", 0, 0, tiled=True)
    return summed.transpose(1, 0, 2).reshape(part // CB, CB * columns)


def solution(mesh):
    named = Mesh(mesh.devices.reshape(ZH, X, Y, C, RG, CB), AXES)
    return jax.shard_map(
        body,
        mesh=named,
        in_specs=(P(DP, None), P(DP, None, MP), P(MP, None)),
        out_specs=P(DP + MP, None),
        check_vma=False,
    )
```

```python
import math

import jax
import jax.numpy as jnp
from jax import lax
from jax.experimental import pallas as pl
from jax.experimental.pallas import tpu as pltpu
from jax.sharding import Mesh
from jax.sharding import PartitionSpec as P

HD = 128
ZH, X, Y, C = 2, 4, 8, 2
XQ, YQ = X // 2, Y // 2
RG, CB = 2, 4
AXES = ("zh", "x", "y", "c", "rg", "cb")
DP, MP = AXES[:4], AXES[4:]


def place(zh, x, y, c):
    return ((zh * X + x % X) * Y + y % Y) * C + c


FAR = [
    [place(zh, 2 * xq + px, 2 * yq + py, c) for xq in range(XQ) for yq in range(YQ)]
    for zh in range(ZH) for c in range(C) for px in range(2) for py in range(2)
]
NEAR = [
    [place(zh, 2 * xq + (1 - 2 * c) * px, 2 * yq + (1 - 2 * c) * py, c) for px in range(2) for py in range(2)]
    for zh in range(ZH) for c in range(C) for xq in range(XQ) for yq in range(YQ)
]


def copies_kernel(block_ref, *refs):
    out_ref, sems = refs[-2:]
    lead = len(out_ref.shape) - len(block_ref.shape) == 1 and out_ref.shape[1:] == block_ref.shape
    moves = [
        pltpu.make_async_copy(block_ref, out_ref.at[i] if lead else out_ref.at[:, i], sems.at[i])
        for i in range(sems.shape[0])
    ]
    for move in moves:
        move.start()
    for move in moves:
        move.wait()


def copies(block, n, axis, after=()):
    anywhere = pl.BlockSpec(memory_space=pl.ANY)
    return pl.pallas_call(
        copies_kernel,
        out_shape=jax.ShapeDtypeStruct(block.shape[:axis] + (n,) + block.shape[axis:], block.dtype),
        in_specs=[anywhere] * (1 + len(after)),
        out_specs=anywhere,
        scratch_shapes=[pltpu.SemaphoreType.DMA((n,))],
        cost_estimate=pl.CostEstimate(flops=0, bytes_accessed=2 * n * block.size, transcendentals=0),
        name="copies",
    )(block, *after)


def spread(block, groups, after=()):
    blocks = copies(block, len(groups[0]), 0, after)
    return lax.all_to_all(blocks, DP, 0, 0, axis_index_groups=groups, tiled=True)


def attend_kernel(own_ref, other_ref, w_ref, *refs):
    out_ref = refs[-1]
    span = Y * w_ref.shape[5]
    totals = [None, None]
    for zh in range(ZH):
        for x in range(X):
            weight = jnp.concatenate(
                [w_ref[x % 2, y % 2, x // 2, y // 2, zh] for y in range(Y)], axis=0
            )
            start = (zh * X + x) * span
            for g, ref in enumerate((own_ref, other_ref)):
                product = jnp.dot(
                    ref[:, start : start + span], weight, preferred_element_type=jnp.float32
                )
                totals[g] = product if totals[g] is None else totals[g] + product
    for g in range(2):
        projected = totals[g].astype(jnp.bfloat16)
        queries, key_rows, values = (projected[:, i * HD : (i + 1) * HD] for i in range(3))
        scores = lax.dot_general(
            queries, key_rows, (((1,), (1,)), ((), ())), preferred_element_type=jnp.float32
        ) * (1.0 / math.sqrt(HD))
        raised = jnp.exp(scores - jnp.max(scores, axis=-1, keepdims=True))
        attn = (raised / jnp.sum(raised, axis=-1, keepdims=True)).astype(jnp.bfloat16)
        out_ref[g] = jnp.dot(attn, values, preferred_element_type=jnp.float32).astype(jnp.bfloat16)


def split_kernel(place_ref, w_ref, after_ref, own_ref, *out_refs):
    column, core = place_ref[0], place_ref[1]
    part, width = out_refs[0].shape
    own_ref[...] = w_ref[:, pl.ds(pl.multiple_of(column * width, width), width)]
    rows = pl.ds(pl.multiple_of(core * part, part), part)
    for i, out_ref in enumerate(out_refs):
        start = pl.multiple_of((column ^ (i + 1)) * width, width)
        out_ref[...] = w_ref[rows, pl.ds(start, width)]


def project_kernel(place_ref, mixed_ref, own_ref, held_ref, partner_ref, far_ref, near_ref):
    column, half, core = place_ref[0], place_ref[1], place_ref[2]
    rows = far_ref.shape[0]
    for out_ref, start in ((far_ref, (1 - half) * rows), (near_ref, half * rows)):
        span = pl.ds(pl.multiple_of(start, rows), rows)
        mixed = jnp.concatenate([mixed_ref[c, column, span] for c in range(C)], axis=1)
        term = jnp.dot(mixed, own_ref[...], preferred_element_type=jnp.float32).astype(jnp.bfloat16)
        total = term.astype(jnp.float32)
        for i in range(CB - 1):
            block = column ^ (i + 1)
            mixed = jnp.concatenate([mixed_ref[core, block, span], mixed_ref[1 - core, block, span]], axis=1)
            weight = jnp.concatenate([held_ref[i], partner_ref[i]], axis=0)
            term = jnp.dot(mixed, weight, preferred_element_type=jnp.float32).astype(jnp.bfloat16)
            total += term.astype(jnp.float32)
        out_ref[...] = total.astype(out_ref.dtype)


def body(tokens, qkv_weight, out_weight):
    rows, width = tokens.shape
    k_rows = qkv_weight.shape[0]
    other = lax.ppermute(tokens, "c", [(0, 1), (1, 0)])

    heads = qkv_weight.reshape(k_rows, 3, C, HD).transpose(2, 0, 1, 3).reshape(C, k_rows, 3 * HD)
    heads = jnp.broadcast_to(heads[None], (ZH,) + heads.shape).reshape(ZH * C, k_rows, 3 * HD)
    heads = lax.all_to_all(heads, ("zh", "c"), 0, 0, tiled=True)
    first = heads
    heads = spread(heads, FAR)

    column, half, core = lax.axis_index("cb"), lax.axis_index("rg"), lax.axis_index("c")
    depth, columns = out_weight.shape[0], out_weight.shape[1] // CB
    smem, vmem = pl.BlockSpec(memory_space=pltpu.SMEM), pl.BlockSpec(memory_space=pltpu.VMEM)
    own_weight, *sent = pl.pallas_call(
        split_kernel,
        out_shape=[jax.ShapeDtypeStruct((depth, columns), jnp.bfloat16)]
        + [jax.ShapeDtypeStruct((depth // C, columns), jnp.bfloat16)] * (CB - 1),
        in_specs=[smem, vmem, vmem],
        out_specs=[vmem] * CB,
        compiler_params=pltpu.CompilerParams(vmem_limit_bytes=24 << 20),
        cost_estimate=pl.CostEstimate(flops=0, bytes_accessed=4 << 20, transcendentals=0),
        name="split",
    )(jnp.stack([column, core]), out_weight, first)
    held = [lax.ppermute(block, "cb", [(j, j ^ (i + 1)) for j in range(CB)]) for i, block in enumerate(sent)]

    heads = spread(heads, NEAR, held[:2]).reshape(2, 2, XQ, YQ, ZH, C * k_rows, 3 * HD)

    mixed = pl.pallas_call(
        attend_kernel,
        out_shape=jax.ShapeDtypeStruct((2, rows, HD), jnp.bfloat16),
        in_specs=[vmem] * 3 + [pl.BlockSpec(memory_space=pl.ANY)],
        compiler_params=pltpu.CompilerParams(vmem_limit_bytes=48 << 20),
        cost_estimate=pl.CostEstimate(flops=2 * 2 * rows * width * 3 * HD, bytes_accessed=8 << 20, transcendentals=0),
        name="attend",
    )(tokens, other, heads, held[2])
    held = jnp.stack(held)
    partner = lax.ppermute(held, "c", [(0, 1), (1, 0)])
    mixed = jnp.where(core == 0, mixed, mixed[::-1])
    mixed = jnp.broadcast_to(mixed[:, None], (C, CB, rows, HD)).reshape(C * CB, rows, HD)
    mixed = lax.all_to_all(mixed, ("c", "cb"), 0, 0, tiled=True).reshape(C, CB, rows, HD)

    part = rows // RG
    far, near = pl.pallas_call(
        project_kernel,
        out_shape=[
            jax.ShapeDtypeStruct((part, columns), jnp.bfloat16),
            jax.ShapeDtypeStruct((part, columns), jnp.float32),
        ],
        in_specs=[smem] + [vmem] * 4,
        out_specs=[vmem] * 2,
        compiler_params=pltpu.CompilerParams(vmem_limit_bytes=24 << 20),
        cost_estimate=pl.CostEstimate(flops=2 * rows * CB * C * HD * columns, bytes_accessed=4 << 20, transcendentals=0),
        name="project",
    )(jnp.stack([column, half, core]), mixed, own_weight, held, partner)
    far = lax.ppermute(far, "rg", [(0, 1), (1, 0)])
    summed = (near + far.astype(jnp.float32)).astype(jnp.bfloat16)
    summed = summed.reshape(CB, part // CB, columns)
    summed = lax.all_to_all(summed, "cb", 0, 0, tiled=True)
    return summed.transpose(1, 0, 2).reshape(part // CB, CB * columns)


def solution(mesh):
    named = Mesh(mesh.devices.reshape(ZH, X, Y, C, RG, CB), AXES)
    return jax.shard_map(
        body,
        mesh=named,
        in_specs=(P(DP, None), P(DP, None, MP), P(MP, None)),
        out_specs=P(DP + MP, None),
        check_vma=False,
    )
```

```python
import math

import jax
import jax.numpy as jnp
from jax import lax
from jax.experimental import pallas as pl
from jax.experimental.pallas import tpu as pltpu
from jax.sharding import Mesh
from jax.sharding import PartitionSpec as P

HD = 128
ZH, X, Y, C = 2, 4, 8, 2
XQ, YQ = X // 2, Y // 2
RG, CB = 2, 4
AXES = ("zh", "x", "y", "c", "rg", "cb")
DP, MP = AXES[:4], AXES[4:]


def place(zh, x, y, c):
    return ((zh * X + x % X) * Y + y % Y) * C + c


FAR = [
    [place(zh, 2 * xq + px, 2 * yq + py, c) for xq in range(XQ) for yq in range(YQ)]
    for zh in range(ZH) for c in range(C) for px in range(2) for py in range(2)
]
NEAR = [
    [
        (
            place(zh, x, y, c),
            place(
                zh,
                x + dx * (1 - 2 * (x % 2)) * (1 - 2 * c),
                y + dy * (1 - 2 * (y % 2)) * (1 - 2 * c),
                c,
            ),
        )
        for zh in range(ZH) for x in range(X) for y in range(Y) for c in range(C)
    ]
    for dx, dy in ((0, 1), (1, 0), (1, 1))
]
ANYWHERE = pl.BlockSpec(memory_space=pl.ANY)


def behind_kernel(*refs):
    pass


def behind(array, after):
    return pl.pallas_call(
        behind_kernel,
        out_shape=jax.ShapeDtypeStruct(array.shape, array.dtype),
        in_specs=[ANYWHERE] * (1 + len(after)),
        out_specs=ANYWHERE,
        input_output_aliases={0: 0},
        name="behind",
    )(array, *after)


def spread(block, groups):
    n = len(groups[0])
    blocks = jnp.broadcast_to(block[None], (n,) + block.shape)
    return lax.all_to_all(blocks, DP, 0, 0, axis_index_groups=groups, tiled=True)


def attend_kernel(place_ref, own_ref, other_ref, *refs):
    w_refs, (out_ref, held_ref, sems) = refs[:4], refs[5:]
    me = place_ref[0]
    for i, w_ref in enumerate(w_refs):
        pltpu.make_async_copy(w_ref, held_ref.at[me ^ i], sems.at[i]).start()
    span = Y * held_ref.shape[4]
    totals = [None, None]
    for px in range(2):
        for slot in (2 * px, 2 * px + 1):
            pltpu.make_async_copy(w_refs[0], held_ref.at[slot], sems.at[me ^ slot]).wait()
        for zh in range(ZH):
            for xq in range(XQ):
                weight = jnp.concatenate(
                    [held_ref[2 * px + y % 2, xq, y // 2, zh] for y in range(Y)], axis=0
                )
                start = (zh * X + 2 * xq + px) * span
                for g, ref in enumerate((own_ref, other_ref)):
                    product = jnp.dot(
                        ref[:, start : start + span], weight, preferred_element_type=jnp.float32
                    )
                    totals[g] = product if totals[g] is None else totals[g] + product
    for g in range(2):
        projected = totals[g].astype(jnp.bfloat16)
        queries, key_rows, values = (projected[:, i * HD : (i + 1) * HD] for i in range(3))
        scores = lax.dot_general(
            queries, key_rows, (((1,), (1,)), ((), ())), preferred_element_type=jnp.float32
        ) * (1.0 / math.sqrt(HD))
        raised = jnp.exp(scores - jnp.max(scores, axis=-1, keepdims=True))
        attn = (raised / jnp.sum(raised, axis=-1, keepdims=True)).astype(jnp.bfloat16)
        out_ref[g] = jnp.dot(attn, values, preferred_element_type=jnp.float32).astype(jnp.bfloat16)


def split_kernel(place_ref, w_ref, after_ref, own_ref, *out_refs):
    column, core = place_ref[0], place_ref[1]
    part, width = out_refs[0].shape
    own_ref[...] = w_ref[:, pl.ds(pl.multiple_of(column * width, width), width)]
    rows = pl.ds(pl.multiple_of(core * part, part), part)
    for i, out_ref in enumerate(out_refs):
        start = pl.multiple_of((column ^ (i + 1)) * width, width)
        out_ref[...] = w_ref[rows, pl.ds(start, width)]


def project_kernel(place_ref, mixed_ref, own_ref, held_ref, partner_ref, far_ref, near_ref):
    column, half, core = place_ref[0], place_ref[1], place_ref[2]
    rows = far_ref.shape[0]
    for out_ref, start in ((far_ref, (1 - half) * rows), (near_ref, half * rows)):
        span = pl.ds(pl.multiple_of(start, rows), rows)
        mixed = jnp.concatenate([mixed_ref[c, column, span] for c in range(C)], axis=1)
        term = jnp.dot(mixed, own_ref[...], preferred_element_type=jnp.float32).astype(jnp.bfloat16)
        total = term.astype(jnp.float32)
        for i in range(CB - 1):
            block = column ^ (i + 1)
            mixed = jnp.concatenate([mixed_ref[core, block, span], mixed_ref[1 - core, block, span]], axis=1)
            weight = jnp.concatenate([held_ref[i], partner_ref[i]], axis=0)
            term = jnp.dot(mixed, weight, preferred_element_type=jnp.float32).astype(jnp.bfloat16)
            total += term.astype(jnp.float32)
        out_ref[...] = total.astype(out_ref.dtype)


def body(tokens, qkv_weight, out_weight):
    rows, width = tokens.shape
    k_rows = qkv_weight.shape[0]
    other = lax.ppermute(tokens, "c", [(0, 1), (1, 0)])

    heads = qkv_weight.reshape(k_rows, 3, C, HD).transpose(2, 0, 1, 3).reshape(C, k_rows, 3 * HD)
    heads = jnp.broadcast_to(heads[None], (ZH,) + heads.shape).reshape(ZH * C, k_rows, 3 * HD)
    heads = lax.all_to_all(heads, ("zh", "c"), 0, 0, tiled=True)
    first = heads
    heads = spread(heads, FAR)

    column, half, core = lax.axis_index("cb"), lax.axis_index("rg"), lax.axis_index("c")
    depth, columns = out_weight.shape[0], out_weight.shape[1] // CB
    smem, vmem = pl.BlockSpec(memory_space=pltpu.SMEM), pl.BlockSpec(memory_space=pltpu.VMEM)
    own_weight, *sent = pl.pallas_call(
        split_kernel,
        out_shape=[jax.ShapeDtypeStruct((depth, columns), jnp.bfloat16)]
        + [jax.ShapeDtypeStruct((depth // C, columns), jnp.bfloat16)] * (CB - 1),
        in_specs=[smem, vmem, vmem],
        out_specs=[vmem] * CB,
        compiler_params=pltpu.CompilerParams(vmem_limit_bytes=24 << 20),
        cost_estimate=pl.CostEstimate(flops=0, bytes_accessed=4 << 20, transcendentals=0),
        name="split",
    )(jnp.stack([column, core]), out_weight, first)
    held = [lax.ppermute(block, "cb", [(j, j ^ (i + 1)) for j in range(CB)]) for i, block in enumerate(sent)]

    heads = behind(heads, held[:2]).reshape(XQ, YQ, ZH, C * k_rows, 3 * HD)
    squares = [heads] + [lax.ppermute(heads, DP, pairs) for pairs in NEAR]
    parity = lax.axis_index("x") % 2 * 2 + lax.axis_index("y") % 2

    mixed = pl.pallas_call(
        attend_kernel,
        out_shape=jax.ShapeDtypeStruct((2, rows, HD), jnp.bfloat16),
        in_specs=[smem] + [vmem] * 2 + [ANYWHERE] * 5,
        scratch_shapes=[pltpu.VMEM((4,) + heads.shape, jnp.bfloat16), pltpu.SemaphoreType.DMA((4,))],
        compiler_params=pltpu.CompilerParams(vmem_limit_bytes=48 << 20),
        cost_estimate=pl.CostEstimate(flops=2 * 2 * rows * width * 3 * HD, bytes_accessed=8 << 20, transcendentals=0),
        name="attend",
    )(parity[None], tokens, other, *squares, held[2])
    held = jnp.stack(held)
    partner = lax.ppermute(held, "c", [(0, 1), (1, 0)])
    mixed = jnp.where(core == 0, mixed, mixed[::-1])
    mixed = jnp.broadcast_to(mixed[:, None], (C, CB, rows, HD)).reshape(C * CB, rows, HD)
    mixed = lax.all_to_all(mixed, ("c", "cb"), 0, 0, tiled=True).reshape(C, CB, rows, HD)

    part = rows // RG
    far, near = pl.pallas_call(
        project_kernel,
        out_shape=[
            jax.ShapeDtypeStruct((part, columns), jnp.bfloat16),
            jax.ShapeDtypeStruct((part, columns), jnp.float32),
        ],
        in_specs=[smem] + [vmem] * 4,
        out_specs=[vmem] * 2,
        compiler_params=pltpu.CompilerParams(vmem_limit_bytes=24 << 20),
        cost_estimate=pl.CostEstimate(flops=2 * rows * CB * C * HD * columns, bytes_accessed=4 << 20, transcendentals=0),
        name="project",
    )(jnp.stack([column, half, core]), mixed, own_weight, held, partner)
    far = lax.ppermute(far, "rg", [(0, 1), (1, 0)])
    summed = (near + far.astype(jnp.float32)).astype(jnp.bfloat16)
    summed = summed.reshape(CB, part // CB, columns)
    summed = lax.all_to_all(summed, "cb", 0, 0, tiled=True)
    return summed.transpose(1, 0, 2).reshape(part // CB, CB * columns)


def solution(mesh):
    named = Mesh(mesh.devices.reshape(ZH, X, Y, C, RG, CB), AXES)
    return jax.shard_map(
        body,
        mesh=named,
        in_specs=(P(DP, None), P(DP, None, MP), P(MP, None)),
        out_specs=P(DP + MP, None),
        check_vma=False,
    )
```

```python
import math

import jax
import jax.numpy as jnp
from jax import lax
from jax.experimental import pallas as pl
from jax.experimental.pallas import tpu as pltpu
from jax.sharding import Mesh
from jax.sharding import PartitionSpec as P

HD = 128
ZH, X, Y, C = 2, 4, 8, 2
XQ, YQ = X // 2, Y // 2
RG, CB = 2, 4
AXES = ("zh", "x", "y", "c", "rg", "cb")
DP, MP = AXES[:4], AXES[4:]


def place(zh, x, y, c):
    return ((zh * X + x % X) * Y + y % Y) * C + c


FAR = [
    [place(zh, 2 * xq + px, 2 * yq + py, c) for xq in range(XQ) for yq in range(YQ)]
    for zh in range(ZH) for c in range(C) for px in range(2) for py in range(2)
]
NEAR = [
    [
        (
            place(zh, x, y, c),
            place(
                zh,
                x + dx * (1 - 2 * (x % 2)) * (1 - 2 * c),
                y + dy * (1 - 2 * (y % 2)) * (1 - 2 * c),
                c,
            ),
        )
        for zh in range(ZH) for x in range(X) for y in range(Y) for c in range(C)
    ]
    for dx, dy in ((0, 1), (1, 0), (1, 1))
]
ANYWHERE = pl.BlockSpec(memory_space=pl.ANY)


def behind_kernel(*refs):
    pass


def behind(array, after):
    return pl.pallas_call(
        behind_kernel,
        out_shape=jax.ShapeDtypeStruct(array.shape, array.dtype),
        in_specs=[ANYWHERE] * (1 + len(after)),
        out_specs=ANYWHERE,
        input_output_aliases={0: 0},
        name="behind",
    )(array, *after)


def copies_kernel(block_ref, after_ref, out_ref):
    for i in range(out_ref.shape[0]):
        out_ref[i] = block_ref[...]


def spread(block, groups, after):
    vmem = pl.BlockSpec(memory_space=pltpu.VMEM)
    blocks = pl.pallas_call(
        copies_kernel,
        out_shape=jax.ShapeDtypeStruct((len(groups[0]),) + block.shape, block.dtype),
        in_specs=[vmem, ANYWHERE],
        out_specs=vmem,
        name="copies",
    )(block, after)
    return lax.all_to_all(blocks, DP, 0, 0, axis_index_groups=groups, tiled=True)


def attend_kernel(place_ref, own_ref, other_ref, *refs):
    w_refs, (out_ref, held_ref, sems) = refs[:4], refs[5:]
    me = place_ref[0]
    for i, w_ref in enumerate(w_refs):
        pltpu.make_async_copy(w_ref, held_ref.at[me ^ i], sems.at[i]).start()
    span = Y * held_ref.shape[4]
    totals = [None, None]
    for px in range(2):
        for slot in (2 * px, 2 * px + 1):
            pltpu.make_async_copy(w_refs[0], held_ref.at[slot], sems.at[me ^ slot]).wait()
        for zh in range(ZH):
            for xq in range(XQ):
                weight = jnp.concatenate(
                    [held_ref[2 * px + y % 2, xq, y // 2, zh] for y in range(Y)], axis=0
                )
                start = (zh * X + 2 * xq + px) * span
                for g, ref in enumerate((own_ref, other_ref)):
                    product = jnp.dot(
                        ref[:, start : start + span], weight, preferred_element_type=jnp.float32
                    )
                    totals[g] = product if totals[g] is None else totals[g] + product
    for g in range(2):
        projected = totals[g].astype(jnp.bfloat16)
        queries, key_rows, values = (projected[:, i * HD : (i + 1) * HD] for i in range(3))
        scores = lax.dot_general(
            queries, key_rows, (((1,), (1,)), ((), ())), preferred_element_type=jnp.float32
        ) * (1.0 / math.sqrt(HD))
        raised = jnp.exp(scores - jnp.max(scores, axis=-1, keepdims=True))
        attn = (raised / jnp.sum(raised, axis=-1, keepdims=True)).astype(jnp.bfloat16)
        out_ref[g] = jnp.dot(attn, values, preferred_element_type=jnp.float32).astype(jnp.bfloat16)


def split_kernel(place_ref, w_ref, own_ref, *out_refs):
    column, core = place_ref[0], place_ref[1]
    part, width = out_refs[0].shape
    own_ref[...] = w_ref[:, pl.ds(pl.multiple_of(column * width, width), width)]
    rows = pl.ds(pl.multiple_of(core * part, part), part)
    for i, out_ref in enumerate(out_refs):
        start = pl.multiple_of((column ^ (i + 1)) * width, width)
        out_ref[...] = w_ref[rows, pl.ds(start, width)]


def project_kernel(place_ref, mixed_ref, own_ref, held_ref, partner_ref, far_ref, near_ref):
    column, half, core = place_ref[0], place_ref[1], place_ref[2]
    rows = far_ref.shape[0]
    for out_ref, start in ((far_ref, (1 - half) * rows), (near_ref, half * rows)):
        span = pl.ds(pl.multiple_of(start, rows), rows)
        mixed = jnp.concatenate([mixed_ref[c, column, span] for c in range(C)], axis=1)
        term = jnp.dot(mixed, own_ref[...], preferred_element_type=jnp.float32).astype(jnp.bfloat16)
        total = term.astype(jnp.float32)
        for i in range(CB - 1):
            block = column ^ (i + 1)
            mixed = jnp.concatenate([mixed_ref[core, block, span], mixed_ref[1 - core, block, span]], axis=1)
            weight = jnp.concatenate([held_ref[i], partner_ref[i]], axis=0)
            term = jnp.dot(mixed, weight, preferred_element_type=jnp.float32).astype(jnp.bfloat16)
            total += term.astype(jnp.float32)
        out_ref[...] = total.astype(out_ref.dtype)


def body(tokens, qkv_weight, out_weight):
    rows, width = tokens.shape
    k_rows = qkv_weight.shape[0]
    other = lax.ppermute(tokens, "c", [(0, 1), (1, 0)])

    heads = qkv_weight.reshape(k_rows, 3, C, HD).transpose(2, 0, 1, 3).reshape(C, k_rows, 3 * HD)
    heads = jnp.broadcast_to(heads[None], (ZH,) + heads.shape).reshape(ZH * C, k_rows, 3 * HD)
    heads = lax.all_to_all(heads, ("zh", "c"), 0, 0, tiled=True)

    column, half, core = lax.axis_index("cb"), lax.axis_index("rg"), lax.axis_index("c")
    depth, columns = out_weight.shape[0], out_weight.shape[1] // CB
    smem, vmem = pl.BlockSpec(memory_space=pltpu.SMEM), pl.BlockSpec(memory_space=pltpu.VMEM)
    own_weight, *sent = pl.pallas_call(
        split_kernel,
        out_shape=[jax.ShapeDtypeStruct((depth, columns), jnp.bfloat16)]
        + [jax.ShapeDtypeStruct((depth // C, columns), jnp.bfloat16)] * (CB - 1),
        in_specs=[smem, vmem],
        out_specs=[vmem] * CB,
        compiler_params=pltpu.CompilerParams(vmem_limit_bytes=24 << 20),
        cost_estimate=pl.CostEstimate(flops=0, bytes_accessed=4 << 20, transcendentals=0),
        name="split",
    )(jnp.stack([column, core]), out_weight)
    held = [lax.ppermute(block, "cb", [(j, j ^ (i + 1)) for j in range(CB)]) for i, block in enumerate(sent)]

    heads = spread(heads, FAR, held[0])
    heads = behind(heads, held[1:2]).reshape(XQ, YQ, ZH, C * k_rows, 3 * HD)
    squares = [heads] + [lax.ppermute(heads, DP, pairs) for pairs in NEAR]
    parity = lax.axis_index("x") % 2 * 2 + lax.axis_index("y") % 2

    mixed = pl.pallas_call(
        attend_kernel,
        out_shape=jax.ShapeDtypeStruct((2, rows, HD), jnp.bfloat16),
        in_specs=[smem] + [vmem] * 2 + [ANYWHERE] * 5,
        scratch_shapes=[pltpu.VMEM((4,) + heads.shape, jnp.bfloat16), pltpu.SemaphoreType.DMA((4,))],
        compiler_params=pltpu.CompilerParams(vmem_limit_bytes=48 << 20),
        cost_estimate=pl.CostEstimate(flops=2 * 2 * rows * width * 3 * HD, bytes_accessed=8 << 20, transcendentals=0),
        name="attend",
    )(parity[None], tokens, other, *squares, held[2])
    held = jnp.stack(held)
    partner = lax.ppermute(held, "c", [(0, 1), (1, 0)])
    mixed = jnp.where(core == 0, mixed, mixed[::-1])
    mixed = jnp.broadcast_to(mixed[:, None], (C, CB, rows, HD)).reshape(C * CB, rows, HD)
    mixed = lax.all_to_all(mixed, ("c", "cb"), 0, 0, tiled=True).reshape(C, CB, rows, HD)

    part = rows // RG
    far, near = pl.pallas_call(
        project_kernel,
        out_shape=[
            jax.ShapeDtypeStruct((part, columns), jnp.bfloat16),
            jax.ShapeDtypeStruct((part, columns), jnp.float32),
        ],
        in_specs=[smem] + [vmem] * 4,
        out_specs=[vmem] * 2,
        compiler_params=pltpu.CompilerParams(vmem_limit_bytes=24 << 20),
        cost_estimate=pl.CostEstimate(flops=2 * rows * CB * C * HD * columns, bytes_accessed=4 << 20, transcendentals=0),
        name="project",
    )(jnp.stack([column, half, core]), mixed, own_weight, held, partner)
    far = lax.ppermute(far, "rg", [(0, 1), (1, 0)])
    summed = (near + far.astype(jnp.float32)).astype(jnp.bfloat16)
    summed = summed.reshape(CB, part // CB, columns)
    summed = lax.all_to_all(summed, "cb", 0, 0, tiled=True)
    return summed.transpose(1, 0, 2).reshape(part // CB, CB * columns)


def solution(mesh):
    named = Mesh(mesh.devices.reshape(ZH, X, Y, C, RG, CB), AXES)
    return jax.shard_map(
        body,
        mesh=named,
        in_specs=(P(DP, None), P(DP, None, MP), P(MP, None)),
        out_specs=P(DP + MP, None),
        check_vma=False,
    )
```

```python
import math

import jax
import jax.numpy as jnp
from jax import lax
from jax.experimental import pallas as pl
from jax.experimental.pallas import tpu as pltpu
from jax.sharding import Mesh
from jax.sharding import PartitionSpec as P

HD = 128
ZH, X, Y, C = 2, 4, 8, 2
XQ, YQ = X // 2, Y // 2
RG, CB = 2, 4
AXES = ("zh", "x", "y", "c", "rg", "cb")
DP, MP = AXES[:4], AXES[4:]


def place(zh, x, y, c):
    return ((zh * X + x % X) * Y + y % Y) * C + c


FAR = [
    [place(zh, 2 * xq + px, 2 * yq + py, c) for xq in range(XQ) for yq in range(YQ)]
    for zh in range(ZH) for c in range(C) for px in range(2) for py in range(2)
]
NEAR = [
    [
        (
            place(zh, x, y, c),
            place(
                zh,
                x + dx * (1 - 2 * (x % 2)) * (1 - 2 * c),
                y + dy * (1 - 2 * (y % 2)) * (1 - 2 * c),
                c,
            ),
        )
        for zh in range(ZH) for x in range(X) for y in range(Y) for c in range(C)
    ]
    for dx, dy in ((0, 1), (1, 0), (1, 1))
]
ANYWHERE = pl.BlockSpec(memory_space=pltpu.HBM)


def behind_kernel(*refs):
    pass


def behind(array, after):
    return pl.pallas_call(
        behind_kernel,
        out_shape=jax.ShapeDtypeStruct(array.shape, array.dtype),
        in_specs=[ANYWHERE] * (1 + len(after)),
        out_specs=ANYWHERE,
        input_output_aliases={0: 0},
        name="behind",
    )(array, *after)


def spread(block, groups):
    n = len(groups[0])
    blocks = jnp.broadcast_to(block[None], (n,) + block.shape)
    return lax.all_to_all(blocks, DP, 0, 0, axis_index_groups=groups, tiled=True)


def attend_kernel(place_ref, own_ref, other_ref, *refs):
    w_refs, (out_ref, held_ref, sems) = refs[:4], refs[5:]
    me, core = place_ref[0], place_ref[1]
    for i, w_ref in enumerate(w_refs):
        pltpu.make_async_copy(w_ref, held_ref.at[me ^ i], sems.at[i]).start()
    span = Y * held_ref.shape[4]
    totals = [None, None]
    for px in range(2):
        for slot in (2 * px, 2 * px + 1):
            pltpu.make_async_copy(w_refs[0], held_ref.at[slot], sems.at[me ^ slot]).wait()
        for zh in range(ZH):
            for xq in range(XQ):
                weight = jnp.concatenate(
                    [held_ref[2 * px + y % 2, xq, y // 2, zh] for y in range(Y)], axis=0
                )
                start = (zh * X + 2 * xq + px) * span
                for g, ref in enumerate((own_ref, other_ref)):
                    product = jnp.dot(
                        ref[:, start : start + span], weight, preferred_element_type=jnp.float32
                    )
                    totals[g] = product if totals[g] is None else totals[g] + product
    for g in range(2):
        projected = totals[g].astype(jnp.bfloat16)
        queries, key_rows, values = (projected[:, i * HD : (i + 1) * HD] for i in range(3))
        scores = lax.dot_general(
            queries, key_rows, (((1,), (1,)), ((), ())), preferred_element_type=jnp.float32
        ) * (1.0 / math.sqrt(HD))
        raised = jnp.exp(scores - jnp.max(scores, axis=-1, keepdims=True))
        attn = (raised / jnp.sum(raised, axis=-1, keepdims=True)).astype(jnp.bfloat16)
        mixed = jnp.dot(attn, values, preferred_element_type=jnp.float32).astype(jnp.bfloat16)
        for cb in range(CB):
            out_ref[(core ^ g) * CB + cb] = mixed


def split_kernel(place_ref, w_ref, after_ref, own_ref, *out_refs):
    column, core = place_ref[0], place_ref[1]
    part, width = out_refs[0].shape
    own_ref[...] = w_ref[:, pl.ds(pl.multiple_of(column * width, width), width)]
    rows = pl.ds(pl.multiple_of(core * part, part), part)
    for i, out_ref in enumerate(out_refs):
        start = pl.multiple_of((column ^ (i + 1)) * width, width)
        out_ref[...] = w_ref[rows, pl.ds(start, width)]


def project_kernel(place_ref, mixed_ref, own_ref, held_ref, partner_ref, out_ref):
    column, core = place_ref[0], place_ref[1]
    mixed = jnp.concatenate([mixed_ref[c, column] for c in range(C)], axis=1)
    term = jnp.dot(mixed, own_ref[...], preferred_element_type=jnp.float32).astype(jnp.bfloat16)
    total = term.astype(jnp.float32)
    for i in range(CB - 1):
        block = column ^ (i + 1)
        mixed = jnp.concatenate([mixed_ref[core, block], mixed_ref[1 - core, block]], axis=1)
        weight = jnp.concatenate([held_ref[i], partner_ref[i]], axis=0)
        term = jnp.dot(mixed, weight, preferred_element_type=jnp.float32).astype(jnp.bfloat16)
        total += term.astype(jnp.float32)
    out_ref[...] = total.astype(out_ref.dtype)


def body(tokens, qkv_weight, out_weight):
    rows, width = tokens.shape
    k_rows = qkv_weight.shape[0]
    other = lax.ppermute(tokens, "c", [(0, 1), (1, 0)])

    heads = qkv_weight.reshape(k_rows, 3, C, HD).transpose(2, 0, 1, 3).reshape(C, k_rows, 3 * HD)
    heads = jnp.broadcast_to(heads[None], (ZH,) + heads.shape).reshape(ZH * C, k_rows, 3 * HD)
    heads = lax.all_to_all(heads, ("zh", "c"), 0, 0, tiled=True)
    first = heads
    heads = spread(heads, FAR)

    column, core = lax.axis_index("cb"), lax.axis_index("c")
    depth, columns = out_weight.shape[0], out_weight.shape[1] // CB
    smem, vmem = pl.BlockSpec(memory_space=pltpu.SMEM), pl.BlockSpec(memory_space=pltpu.VMEM)
    own_weight, *sent = pl.pallas_call(
        split_kernel,
        out_shape=[jax.ShapeDtypeStruct((depth, columns), jnp.bfloat16)]
        + [jax.ShapeDtypeStruct((depth // C, columns), jnp.bfloat16)] * (CB - 1),
        in_specs=[smem, vmem, vmem],
        out_specs=[vmem] * CB,
        compiler_params=pltpu.CompilerParams(vmem_limit_bytes=24 << 20),
        cost_estimate=pl.CostEstimate(flops=0, bytes_accessed=4 << 20, transcendentals=0),
        name="split",
    )(jnp.stack([column, core]), out_weight, first)
    held = [lax.ppermute(block, "cb", [(j, j ^ (i + 1)) for j in range(CB)]) for i, block in enumerate(sent)]

    heads = behind(heads, held[:2]).reshape(XQ, YQ, ZH, C * k_rows, 3 * HD)
    squares = [heads] + [lax.ppermute(heads, DP, pairs) for pairs in NEAR]
    parity = lax.axis_index("x") % 2 * 2 + lax.axis_index("y") % 2

    mixed = pl.pallas_call(
        attend_kernel,
        out_shape=jax.ShapeDtypeStruct((C * CB, rows, HD), jnp.bfloat16),
        in_specs=[smem] + [vmem] * 2 + [ANYWHERE] * 5,
        scratch_shapes=[pltpu.VMEM((4,) + heads.shape, jnp.bfloat16), pltpu.SemaphoreType.DMA((4,))],
        compiler_params=pltpu.CompilerParams(vmem_limit_bytes=48 << 20),
        cost_estimate=pl.CostEstimate(flops=2 * 2 * rows * width * 3 * HD, bytes_accessed=8 << 20, transcendentals=0),
        name="attend",
    )(jnp.stack([parity, core]), tokens, other, *squares, held[2])
    held = jnp.stack(held)
    partner = lax.ppermute(held, "c", [(0, 1), (1, 0)])
    mixed = lax.all_to_all(mixed, ("c", "cb"), 0, 0, tiled=True).reshape(C, CB, rows, HD)

    summed = pl.pallas_call(
        project_kernel,
        out_shape=jax.ShapeDtypeStruct((rows, columns), jnp.bfloat16),
        in_specs=[smem] + [vmem] * 4,
        out_specs=vmem,
        compiler_params=pltpu.CompilerParams(vmem_limit_bytes=24 << 20),
        cost_estimate=pl.CostEstimate(flops=2 * rows * CB * C * HD * columns, bytes_accessed=4 << 20, transcendentals=0),
        name="project",
    )(jnp.stack([column, core]), mixed, own_weight, held, partner)
    part = rows // (RG * CB)
    summed = lax.all_to_all(summed.reshape(RG * CB, part, columns), MP, 0, 0, tiled=True)
    summed = summed.reshape(RG, CB, part, columns).astype(jnp.float32)
    summed = (summed[0] + summed[1]).astype(jnp.bfloat16)
    return summed.transpose(1, 0, 2).reshape(part, CB * columns)


def solution(mesh):
    named = Mesh(mesh.devices.reshape(ZH, X, Y, C, RG, CB), AXES)
    return jax.shard_map(
        body,
        mesh=named,
        in_specs=(P(DP, None), P(DP, None, MP), P(MP, None)),
        out_specs=P(DP + MP, None),
        check_vma=False,
    )
```

```python
import math

import jax
import jax.numpy as jnp
from jax import lax
from jax.experimental import pallas as pl
from jax.experimental.pallas import tpu as pltpu
from jax.sharding import Mesh
from jax.sharding import PartitionSpec as P

HD = 128
ZH, X, Y, C = 2, 4, 8, 2
XQ, YQ = X // 2, Y // 2
RG, CB = 2, 4
AXES = ("zh", "x", "y", "c", "rg", "cb")
DP, MP = AXES[:4], AXES[4:]


def place(zh, x, y, c):
    return ((zh * X + x % X) * Y + y % Y) * C + c


FAR = [
    [place(zh, 2 * xq + px, 2 * yq + py, c) for xq in range(XQ) for yq in range(YQ)]
    for zh in range(ZH) for c in range(C) for px in range(2) for py in range(2)
]
NEAR = [
    [
        (
            place(zh, x, y, c),
            place(
                zh,
                x + dx * (1 - 2 * (x % 2)) * (1 - 2 * c),
                y + dy * (1 - 2 * (y % 2)) * (1 - 2 * c),
                c,
            ),
        )
        for zh in range(ZH) for x in range(X) for y in range(Y) for c in range(C)
    ]
    for dx, dy in ((0, 1), (1, 0), (1, 1))
]
ANYWHERE = pl.BlockSpec(memory_space=pltpu.HBM)


def behind_kernel(*refs):
    pass


def behind(array, after):
    return pl.pallas_call(
        behind_kernel,
        out_shape=jax.ShapeDtypeStruct(array.shape, array.dtype),
        in_specs=[ANYWHERE] * (1 + len(after)),
        out_specs=ANYWHERE,
        input_output_aliases={0: 0},
        name="behind",
    )(array, *after)


def spread(block, groups):
    n = len(groups[0])
    blocks = jnp.broadcast_to(block[None], (n,) + block.shape)
    return lax.all_to_all(blocks, DP, 0, 0, axis_index_groups=groups, tiled=True)


def attend_kernel(place_ref, own_ref, other_ref, *refs):
    w_refs, (out_ref, held_ref, sems) = refs[:4], refs[5:]
    me, core = place_ref[0], place_ref[1]
    for i, w_ref in enumerate(w_refs):
        pltpu.make_async_copy(w_ref, held_ref.at[me ^ i], sems.at[i]).start()
    span = Y * held_ref.shape[4]
    totals = [None, None]
    for px in range(2):
        for slot in (2 * px, 2 * px + 1):
            pltpu.make_async_copy(w_refs[0], held_ref.at[slot], sems.at[me ^ slot]).wait()
        for zh in range(ZH):
            for xq in range(XQ):
                weight = jnp.concatenate(
                    [held_ref[2 * px + y % 2, xq, y // 2, zh] for y in range(Y)], axis=0
                )
                start = (zh * X + 2 * xq + px) * span
                for g, ref in enumerate((own_ref, other_ref)):
                    product = jnp.dot(
                        ref[:, start : start + span], weight, preferred_element_type=jnp.float32
                    )
                    totals[g] = product if totals[g] is None else totals[g] + product
    for g in range(2):
        projected = totals[g].astype(jnp.bfloat16)
        queries, key_rows, values = (projected[:, i * HD : (i + 1) * HD] for i in range(3))
        scores = lax.dot_general(
            queries, key_rows, (((1,), (1,)), ((), ())), preferred_element_type=jnp.float32
        ) * (1.0 / math.sqrt(HD))
        raised = jnp.exp(scores - jnp.max(scores, axis=-1, keepdims=True))
        attn = (raised / jnp.sum(raised, axis=-1, keepdims=True)).astype(jnp.bfloat16)
        mixed = jnp.dot(attn, values, preferred_element_type=jnp.float32).astype(jnp.bfloat16)
        for cb in range(CB):
            out_ref[(core ^ g) * CB + cb] = mixed


def split_kernel(place_ref, w_ref, after_ref, own_ref, *out_refs):
    column, core = place_ref[0], place_ref[1]
    part, width = out_refs[0].shape
    own_ref[...] = w_ref[:, pl.ds(pl.multiple_of(column * width, width), width)]
    rows = pl.ds(pl.multiple_of(core * part, part), part)
    for i, out_ref in enumerate(out_refs):
        start = pl.multiple_of((column ^ (i + 1)) * width, width)
        out_ref[...] = w_ref[rows, pl.ds(start, width)]


def project_kernel(place_ref, mixed_ref, own_ref, held_ref, partner_ref, *refs):
    out_refs, sum_ref = refs[:-1], refs[-1]
    column, core, spot = place_ref[0], place_ref[1], place_ref[2]
    mixed = jnp.concatenate([mixed_ref[c, column] for c in range(C)], axis=1)
    term = jnp.dot(mixed, own_ref[...], preferred_element_type=jnp.float32).astype(jnp.bfloat16)
    total = term.astype(jnp.float32)
    for i in range(CB - 1):
        block = column ^ (i + 1)
        mixed = jnp.concatenate([mixed_ref[core, block], mixed_ref[1 - core, block]], axis=1)
        weight = jnp.concatenate([held_ref[i], partner_ref[i]], axis=0)
        term = jnp.dot(mixed, weight, preferred_element_type=jnp.float32).astype(jnp.bfloat16)
        total += term.astype(jnp.float32)
    sum_ref[...] = total.astype(sum_ref.dtype)
    part = out_refs[0].shape[0]
    for i, out_ref in enumerate(out_refs):
        out_ref[...] = sum_ref[pl.ds(pl.multiple_of((spot ^ i) * part, part), part)]


def add_kernel(place_ref, *refs):
    in_refs, out_ref = refs[:-1], refs[-1]
    width = in_refs[0].shape[1]
    for i in range(CB):
        total = in_refs[i][...].astype(jnp.float32) + in_refs[CB + i][...].astype(jnp.float32)
        out_ref[:, pl.ds(pl.multiple_of((place_ref[0] ^ i) * width, width), width)] = total.astype(out_ref.dtype)


def body(tokens, qkv_weight, out_weight):
    rows, width = tokens.shape
    k_rows = qkv_weight.shape[0]
    other = lax.ppermute(tokens, "c", [(0, 1), (1, 0)])

    heads = qkv_weight.reshape(k_rows, 3, C, HD).transpose(2, 0, 1, 3).reshape(C, k_rows, 3 * HD)
    heads = jnp.broadcast_to(heads[None], (ZH,) + heads.shape).reshape(ZH * C, k_rows, 3 * HD)
    heads = lax.all_to_all(heads, ("zh", "c"), 0, 0, tiled=True)
    first = heads
    heads = spread(heads, FAR)

    column, core = lax.axis_index("cb"), lax.axis_index("c")
    depth, columns = out_weight.shape[0], out_weight.shape[1] // CB
    smem, vmem = pl.BlockSpec(memory_space=pltpu.SMEM), pl.BlockSpec(memory_space=pltpu.VMEM)
    own_weight, *sent = pl.pallas_call(
        split_kernel,
        out_shape=[jax.ShapeDtypeStruct((depth, columns), jnp.bfloat16)]
        + [jax.ShapeDtypeStruct((depth // C, columns), jnp.bfloat16)] * (CB - 1),
        in_specs=[smem, vmem, vmem],
        out_specs=[vmem] * CB,
        compiler_params=pltpu.CompilerParams(vmem_limit_bytes=24 << 20),
        cost_estimate=pl.CostEstimate(flops=0, bytes_accessed=4 << 20, transcendentals=0),
        name="split",
    )(jnp.stack([column, core]), out_weight, first)
    held = [lax.ppermute(block, "cb", [(j, j ^ (i + 1)) for j in range(CB)]) for i, block in enumerate(sent)]

    heads = behind(heads, held[:2]).reshape(XQ, YQ, ZH, C * k_rows, 3 * HD)
    squares = [heads] + [lax.ppermute(heads, DP, pairs) for pairs in NEAR]
    parity = lax.axis_index("x") % 2 * 2 + lax.axis_index("y") % 2

    mixed = pl.pallas_call(
        attend_kernel,
        out_shape=jax.ShapeDtypeStruct((C * CB, rows, HD), jnp.bfloat16),
        in_specs=[smem] + [vmem] * 2 + [ANYWHERE] * 5,
        scratch_shapes=[pltpu.VMEM((4,) + heads.shape, jnp.bfloat16), pltpu.SemaphoreType.DMA((4,))],
        compiler_params=pltpu.CompilerParams(vmem_limit_bytes=48 << 20),
        cost_estimate=pl.CostEstimate(flops=2 * 2 * rows * width * 3 * HD, bytes_accessed=8 << 20, transcendentals=0),
        name="attend",
    )(jnp.stack([parity, core]), tokens, other, *squares, held[2])
    held = jnp.stack(held)
    partner = lax.ppermute(held, "c", [(0, 1), (1, 0)])
    mixed = lax.all_to_all(mixed, ("c", "cb"), 0, 0, tiled=True).reshape(C, CB, rows, HD)

    n_mp = RG * CB
    part = rows // n_mp
    spot = jnp.stack([column, core, lax.axis_index("rg") * CB + column])
    sums = pl.pallas_call(
        project_kernel,
        out_shape=[jax.ShapeDtypeStruct((part, columns), jnp.bfloat16)] * n_mp,
        in_specs=[smem] + [vmem] * 4,
        out_specs=[vmem] * n_mp,
        scratch_shapes=[pltpu.VMEM((rows, columns), jnp.bfloat16)],
        compiler_params=pltpu.CompilerParams(vmem_limit_bytes=24 << 20),
        cost_estimate=pl.CostEstimate(flops=2 * rows * CB * C * HD * columns, bytes_accessed=4 << 20, transcendentals=0),
        name="project",
    )(spot, mixed, own_weight, held, partner)
    sums = [sums[0]] + [lax.ppermute(sums[i], MP, [(j, j ^ i) for j in range(n_mp)]) for i in range(1, n_mp)]
    return pl.pallas_call(
        add_kernel,
        out_shape=jax.ShapeDtypeStruct((part, CB * columns), jnp.bfloat16),
        in_specs=[smem] + [vmem] * n_mp,
        out_specs=vmem,
        name="add",
    )(column[None], *sums)


def solution(mesh):
    named = Mesh(mesh.devices.reshape(ZH, X, Y, C, RG, CB), AXES)
    return jax.shard_map(
        body,
        mesh=named,
        in_specs=(P(DP, None), P(DP, None, MP), P(MP, None)),
        out_specs=P(DP + MP, None),
        check_vma=False,
    )
```

```python
import math

import jax
import jax.numpy as jnp
from jax import lax
from jax.experimental import pallas as pl
from jax.experimental.pallas import tpu as pltpu
from jax.sharding import Mesh
from jax.sharding import PartitionSpec as P

HD = 128
ZH, X, Y, C = 2, 4, 8, 2
XQ, YQ = X // 2, Y // 2
RG, CB = 2, 4
AXES = ("zh", "x", "y", "c", "rg", "cb")
DP, MP = AXES[:4], AXES[4:]


def place(zh, x, y, c):
    return ((zh * X + x % X) * Y + y % Y) * C + c


FAR = [
    [place(zh, 2 * xq + px, 2 * yq + py, c) for xq in range(XQ) for yq in range(YQ)]
    for zh in range(ZH) for c in range(C) for px in range(2) for py in range(2)
]
NEAR = [
    [
        (
            place(zh, x, y, c),
            place(
                zh,
                x + dx * (1 - 2 * (x % 2)) * (1 - 2 * c),
                y + dy * (1 - 2 * (y % 2)) * (1 - 2 * c),
                c,
            ),
        )
        for zh in range(ZH) for x in range(X) for y in range(Y) for c in range(C)
    ]
    for dx, dy in ((0, 1), (1, 0), (1, 1))
]
ANYWHERE = pl.BlockSpec(memory_space=pltpu.HBM)


def behind_kernel(*refs):
    pass


def behind(array, after):
    return pl.pallas_call(
        behind_kernel,
        out_shape=jax.ShapeDtypeStruct(array.shape, array.dtype),
        in_specs=[ANYWHERE] * (1 + len(after)),
        out_specs=ANYWHERE,
        input_output_aliases={0: 0},
        name="behind",
    )(array, *after)


def spread(block, groups):
    n = len(groups[0])
    blocks = jnp.broadcast_to(block[None], (n,) + block.shape)
    return lax.all_to_all(blocks, DP, 0, 0, axis_index_groups=groups, tiled=True)


def attend_kernel(place_ref, own_ref, other_ref, *refs):
    w_refs, (out_ref, held_ref, sems) = refs[:4], refs[5:]
    me, core = place_ref[0], place_ref[1]
    for i in range(1, 4):
        pltpu.make_async_copy(w_refs[i], held_ref.at[me ^ i], sems.at[me ^ i]).start()
    held_ref[me] = w_refs[0][...]
    span = Y * held_ref.shape[4]
    totals = [None, None]
    for px in range(2):
        for slot in (2 * px, 2 * px + 1):

            @pl.when(slot != me)
            def _():
                pltpu.make_async_copy(w_refs[1], held_ref.at[slot], sems.at[slot]).wait()

        for zh in range(ZH):
            for xq in range(XQ):
                weight = jnp.concatenate(
                    [held_ref[2 * px + y % 2, xq, y // 2, zh] for y in range(Y)], axis=0
                )
                start = (zh * X + 2 * xq + px) * span
                for g, ref in enumerate((own_ref, other_ref)):
                    product = jnp.dot(
                        ref[:, start : start + span], weight, preferred_element_type=jnp.float32
                    )
                    totals[g] = product if totals[g] is None else totals[g] + product
    for g in range(2):
        projected = totals[g].astype(jnp.bfloat16)
        queries, key_rows, values = (projected[:, i * HD : (i + 1) * HD] for i in range(3))
        scores = lax.dot_general(
            queries, key_rows, (((1,), (1,)), ((), ())), preferred_element_type=jnp.float32
        ) * (1.0 / math.sqrt(HD))
        raised = jnp.exp(scores - jnp.max(scores, axis=-1, keepdims=True))
        attn = (raised / jnp.sum(raised, axis=-1, keepdims=True)).astype(jnp.bfloat16)
        mixed = jnp.dot(attn, values, preferred_element_type=jnp.float32).astype(jnp.bfloat16)
        for cb in range(CB):
            out_ref[(core ^ g) * CB + cb] = mixed


def split_kernel(place_ref, w_ref, *refs):
    column, core = place_ref[0], place_ref[1]
    out_refs = refs[1:]
    part, width = out_refs[0].shape
    rows = pl.ds(pl.multiple_of(core * part, part), part)
    for i, out_ref in enumerate(out_refs):
        start = pl.multiple_of((column ^ (i + 1)) * width, width)
        out_ref[...] = w_ref[rows, pl.ds(start, width)]


def project_kernel(place_ref, mixed_ref, w_ref, held_ref, partner_ref, out_ref, own_ref, sem):
    column, core = place_ref[0], place_ref[1]
    width = own_ref.shape[1]
    fetch = pltpu.make_async_copy(
        w_ref.at[:, pl.ds(pl.multiple_of(column * width, width), width)], own_ref, sem
    )
    fetch.start()
    total = None
    for i in range(CB - 1):
        block = column ^ (i + 1)
        mixed = jnp.concatenate([mixed_ref[core, block], mixed_ref[1 - core, block]], axis=1)
        weight = jnp.concatenate([held_ref[i], partner_ref[i]], axis=0)
        term = jnp.dot(mixed, weight, preferred_element_type=jnp.float32).astype(jnp.bfloat16)
        wide = term.astype(jnp.float32)
        total = wide if total is None else total + wide
    fetch.wait()
    mixed = jnp.concatenate([mixed_ref[c, column] for c in range(C)], axis=1)
    term = jnp.dot(mixed, own_ref[...], preferred_element_type=jnp.float32).astype(jnp.bfloat16)
    out_ref[...] = (total + term.astype(jnp.float32)).astype(out_ref.dtype)


def add_kernel(sums_ref, out_ref):
    width = sums_ref.shape[3]
    for cb in range(CB):
        total = sums_ref[0, cb].astype(jnp.float32) + sums_ref[1, cb].astype(jnp.float32)
        out_ref[:, cb * width : (cb + 1) * width] = total.astype(out_ref.dtype)


def body(tokens, qkv_weight, out_weight):
    rows, width = tokens.shape
    k_rows = qkv_weight.shape[0]
    other = lax.ppermute(tokens, "c", [(0, 1), (1, 0)])

    heads = qkv_weight.reshape(k_rows, 3, C, HD).transpose(2, 0, 1, 3).reshape(C, k_rows, 3 * HD)
    heads = jnp.broadcast_to(heads[None], (ZH,) + heads.shape).reshape(ZH * C, k_rows, 3 * HD)
    heads = lax.all_to_all(heads, ("zh", "c"), 0, 0, tiled=True)
    first = heads
    heads = spread(heads, FAR)

    column, core = lax.axis_index("cb"), lax.axis_index("c")
    depth, columns = out_weight.shape[0], out_weight.shape[1] // CB
    smem, vmem = pl.BlockSpec(memory_space=pltpu.SMEM), pl.BlockSpec(memory_space=pltpu.VMEM)
    sent = pl.pallas_call(
        split_kernel,
        out_shape=[jax.ShapeDtypeStruct((depth // C, columns), jnp.bfloat16)] * (CB - 1),
        in_specs=[smem, vmem, vmem],
        out_specs=[vmem] * (CB - 1),
        compiler_params=pltpu.CompilerParams(vmem_limit_bytes=24 << 20),
        cost_estimate=pl.CostEstimate(flops=0, bytes_accessed=4 << 20, transcendentals=0),
        name="split",
    )(jnp.stack([column, core]), out_weight, first)
    held = [lax.ppermute(block, "cb", [(j, j ^ (i + 1)) for j in range(CB)]) for i, block in enumerate(sent)]

    shape = (XQ, YQ, ZH, C * k_rows, 3 * HD)
    sent = behind(heads, held[:2]).reshape(shape)
    heads = heads.reshape(shape)
    squares = [heads] + [lax.ppermute(sent, DP, pairs) for pairs in NEAR]
    parity = lax.axis_index("x") % 2 * 2 + lax.axis_index("y") % 2

    mixed = pl.pallas_call(
        attend_kernel,
        out_shape=jax.ShapeDtypeStruct((C * CB, rows, HD), jnp.bfloat16),
        in_specs=[smem] + [vmem] * 3 + [ANYWHERE] * 4,
        scratch_shapes=[pltpu.VMEM((4,) + heads.shape, jnp.bfloat16), pltpu.SemaphoreType.DMA((4,))],
        compiler_params=pltpu.CompilerParams(vmem_limit_bytes=48 << 20),
        cost_estimate=pl.CostEstimate(flops=2 * 2 * rows * width * 3 * HD, bytes_accessed=8 << 20, transcendentals=0),
        name="attend",
    )(jnp.stack([parity, core]), tokens, other, *squares, held[2])
    held = jnp.stack(held)
    partner = lax.ppermute(held, "c", [(0, 1), (1, 0)])
    mixed = lax.all_to_all(mixed, ("c", "cb"), 0, 0, tiled=True).reshape(C, CB, rows, HD)

    summed = pl.pallas_call(
        project_kernel,
        out_shape=jax.ShapeDtypeStruct((rows, columns), jnp.bfloat16),
        in_specs=[smem, vmem, ANYWHERE, vmem, vmem],
        out_specs=vmem,
        scratch_shapes=[pltpu.VMEM((depth, columns), jnp.bfloat16), pltpu.SemaphoreType.DMA(())],
        compiler_params=pltpu.CompilerParams(vmem_limit_bytes=24 << 20),
        cost_estimate=pl.CostEstimate(flops=2 * rows * CB * C * HD * columns, bytes_accessed=4 << 20, transcendentals=0),
        name="project",
    )(jnp.stack([column, core]), mixed, out_weight, held, partner)
    part = rows // (RG * CB)
    summed = lax.all_to_all(summed.reshape(RG * CB, part, columns), MP, 0, 0, tiled=True)
    return pl.pallas_call(
        add_kernel,
        out_shape=jax.ShapeDtypeStruct((part, CB * columns), jnp.bfloat16),
        in_specs=[vmem],
        out_specs=vmem,
        name="add",
    )(summed.reshape(RG, CB, part, columns))


def solution(mesh):
    named = Mesh(mesh.devices.reshape(ZH, X, Y, C, RG, CB), AXES)
    return jax.shard_map(
        body,
        mesh=named,
        in_specs=(P(DP, None), P(DP, None, MP), P(MP, None)),
        out_specs=P(DP + MP, None),
        check_vma=False,
    )
```

```python
import math

import jax
import jax.numpy as jnp
from jax import lax
from jax.experimental import pallas as pl
from jax.experimental.pallas import tpu as pltpu
from jax.sharding import Mesh
from jax.sharding import PartitionSpec as P

HD = 128
ZH, X, Y, C = 2, 4, 8, 2
XQ, YQ = X // 2, Y // 2
RG, CB = 2, 4
AXES = ("zh", "x", "y", "c", "rg", "cb")
DP, MP = AXES[:4], AXES[4:]


def place(zh, x, y, c):
    return ((zh * X + x % X) * Y + y % Y) * C + c


FAR = [
    [place(zh, 2 * xq + px, 2 * yq + py, c) for xq in range(XQ) for yq in range(YQ)]
    for zh in range(ZH) for c in range(C) for px in range(2) for py in range(2)
]
NEAR = [
    [
        (
            place(zh, x, y, c),
            place(
                zh,
                x + dx * (1 - 2 * (x % 2)) * (1 - 2 * c),
                y + dy * (1 - 2 * (y % 2)) * (1 - 2 * c),
                c,
            ),
        )
        for zh in range(ZH) for x in range(X) for y in range(Y) for c in range(C)
    ]
    for dx, dy in ((0, 1), (1, 0), (1, 1))
]
ANYWHERE = pl.BlockSpec(memory_space=pltpu.HBM)


def behind_kernel(*refs):
    pass


def behind(array, after):
    return pl.pallas_call(
        behind_kernel,
        out_shape=jax.ShapeDtypeStruct(array.shape, array.dtype),
        in_specs=[ANYWHERE] * (1 + len(after)),
        out_specs=ANYWHERE,
        input_output_aliases={0: 0},
        name="behind",
    )(array, *after)


def spread(block, groups):
    n = len(groups[0])
    blocks = jnp.broadcast_to(block[None], (n,) + block.shape)
    return lax.all_to_all(blocks, DP, 0, 0, axis_index_groups=groups, tiled=True)


def cut_kernel(w_ref, out_ref):
    for i in range(out_ref.shape[0]):
        c = i % C
        for part in range(3):
            out_ref[i, :, part * HD : (part + 1) * HD] = w_ref[part, :, c * HD : (c + 1) * HD]


def attend_kernel(place_ref, own_ref, other_ref, *refs):
    w_refs, (out_ref, held_ref, sems) = refs[:4], refs[6:]
    me, core = place_ref[0], place_ref[1]
    for i, w_ref in enumerate(w_refs):
        pltpu.make_async_copy(w_ref, held_ref.at[me ^ i], sems.at[i]).start()
    span = Y * held_ref.shape[4]
    totals = [None, None]
    for px in range(2):
        for slot in (2 * px, 2 * px + 1):
            pltpu.make_async_copy(w_refs[0], held_ref.at[slot], sems.at[me ^ slot]).wait()
        for zh in range(ZH):
            for xq in range(XQ):
                weight = jnp.concatenate(
                    [held_ref[2 * px + y % 2, xq, y // 2, zh] for y in range(Y)], axis=0
                )
                start = (zh * X + 2 * xq + px) * span
                for g, ref in enumerate((own_ref, other_ref)):
                    product = jnp.dot(
                        ref[:, start : start + span], weight, preferred_element_type=jnp.float32
                    )
                    totals[g] = product if totals[g] is None else totals[g] + product
    for g in range(2):
        projected = totals[g].astype(jnp.bfloat16)
        queries, key_rows, values = (projected[:, i * HD : (i + 1) * HD] for i in range(3))
        scores = lax.dot_general(
            queries, key_rows, (((1,), (1,)), ((), ())), preferred_element_type=jnp.float32
        ) * (1.0 / math.sqrt(HD))
        raised = jnp.exp(scores - jnp.max(scores, axis=-1, keepdims=True))
        attn = (raised / jnp.sum(raised, axis=-1, keepdims=True)).astype(jnp.bfloat16)
        mixed = jnp.dot(attn, values, preferred_element_type=jnp.float32).astype(jnp.bfloat16)
        for cb in range(CB):
            out_ref[(core ^ g) * CB + cb] = mixed


def split_kernel(place_ref, w_ref, after_ref, own_ref, *out_refs):
    column, core = place_ref[0], place_ref[1]
    part, width = out_refs[0].shape
    own_ref[...] = w_ref[:, pl.ds(pl.multiple_of(column * width, width), width)]
    rows = pl.ds(pl.multiple_of(core * part, part), part)
    for i, out_ref in enumerate(out_refs):
        start = pl.multiple_of((column ^ (i + 1)) * width, width)
        out_ref[...] = w_ref[rows, pl.ds(start, width)]


def project_kernel(place_ref, mixed_ref, own_ref, held_ref, partner_ref, out_ref):
    column, core = place_ref[0], place_ref[1]
    mixed = jnp.concatenate([mixed_ref[c, column] for c in range(C)], axis=1)
    term = jnp.dot(mixed, own_ref[...], preferred_element_type=jnp.float32).astype(jnp.bfloat16)
    total = term.astype(jnp.float32)
    for i in range(CB - 1):
        block = column ^ (i + 1)
        mixed = jnp.concatenate([mixed_ref[core, block], mixed_ref[1 - core, block]], axis=1)
        weight = jnp.concatenate([held_ref[i], partner_ref[i]], axis=0)
        term = jnp.dot(mixed, weight, preferred_element_type=jnp.float32).astype(jnp.bfloat16)
        total += term.astype(jnp.float32)
    out_ref[...] = total.astype(out_ref.dtype)


def body(tokens, qkv_weight, out_weight):
    rows, width = tokens.shape
    k_rows = qkv_weight.shape[0]
    other = lax.ppermute(tokens, "c", [(0, 1), (1, 0)])

    heads = pl.pallas_call(
        cut_kernel,
        out_shape=jax.ShapeDtypeStruct((ZH * C, k_rows, 3 * HD), jnp.bfloat16),
        in_specs=[pl.BlockSpec(memory_space=pltpu.VMEM)],
        out_specs=pl.BlockSpec(memory_space=pltpu.VMEM),
        name="cut",
    )(qkv_weight.transpose(1, 0, 2))
    heads = lax.all_to_all(heads, ("zh", "c"), 0, 0, tiled=True)
    first = heads
    heads = spread(heads, FAR)

    column, core = lax.axis_index("cb"), lax.axis_index("c")
    depth, columns = out_weight.shape[0], out_weight.shape[1] // CB
    smem, vmem = pl.BlockSpec(memory_space=pltpu.SMEM), pl.BlockSpec(memory_space=pltpu.VMEM)
    own_weight, *sent = pl.pallas_call(
        split_kernel,
        out_shape=[jax.ShapeDtypeStruct((depth, columns), jnp.bfloat16)]
        + [jax.ShapeDtypeStruct((depth // C, columns), jnp.bfloat16)] * (CB - 1),
        in_specs=[smem, vmem, vmem],
        out_specs=[vmem] * CB,
        compiler_params=pltpu.CompilerParams(vmem_limit_bytes=24 << 20),
        cost_estimate=pl.CostEstimate(flops=0, bytes_accessed=4 << 20, transcendentals=0),
        name="split",
    )(jnp.stack([column, core]), out_weight, first)
    held = [lax.ppermute(block, "cb", [(j, j ^ (i + 1)) for j in range(CB)]) for i, block in enumerate(sent)]

    heads = behind(heads, held[1:2]).reshape(XQ, YQ, ZH, C * k_rows, 3 * HD)
    squares = [heads] + [lax.ppermute(heads, DP, pairs) for pairs in NEAR]
    parity = lax.axis_index("x") % 2 * 2 + lax.axis_index("y") % 2

    mixed = pl.pallas_call(
        attend_kernel,
        out_shape=jax.ShapeDtypeStruct((C * CB, rows, HD), jnp.bfloat16),
        in_specs=[smem] + [vmem] * 2 + [ANYWHERE] * 6,
        scratch_shapes=[pltpu.VMEM((4,) + heads.shape, jnp.bfloat16), pltpu.SemaphoreType.DMA((4,))],
        compiler_params=pltpu.CompilerParams(vmem_limit_bytes=48 << 20),
        cost_estimate=pl.CostEstimate(flops=2 * 2 * rows * width * 3 * HD, bytes_accessed=8 << 20, transcendentals=0),
        name="attend",
    )(jnp.stack([parity, core]), tokens, other, *squares, held[0], held[2])
    held = jnp.stack(held)
    partner = lax.ppermute(held, "c", [(0, 1), (1, 0)])
    mixed = lax.all_to_all(mixed, ("c", "cb"), 0, 0, tiled=True).reshape(C, CB, rows, HD)

    summed = pl.pallas_call(
        project_kernel,
        out_shape=jax.ShapeDtypeStruct((rows, columns), jnp.bfloat16),
        in_specs=[smem] + [vmem] * 4,
        out_specs=vmem,
        compiler_params=pltpu.CompilerParams(vmem_limit_bytes=24 << 20),
        cost_estimate=pl.CostEstimate(flops=2 * rows * CB * C * HD * columns, bytes_accessed=4 << 20, transcendentals=0),
        name="project",
    )(jnp.stack([column, core]), mixed, own_weight, held, partner)
    part = rows // (RG * CB)
    summed = lax.all_to_all(summed.reshape(RG * CB, part, columns), MP, 0, 0, tiled=True)
    summed = summed.reshape(RG, CB, part, columns).astype(jnp.float32)
    summed = (summed[0] + summed[1]).astype(jnp.bfloat16)
    return summed.transpose(1, 0, 2).reshape(part, CB * columns)


def solution(mesh):
    named = Mesh(mesh.devices.reshape(ZH, X, Y, C, RG, CB), AXES)
    return jax.shard_map(
        body,
        mesh=named,
        in_specs=(P(DP, None), P(DP, None, MP), P(MP, None)),
        out_specs=P(DP + MP, None),
        check_vma=False,
    )
```

```python
import math

import jax
import jax.numpy as jnp
from jax import lax
from jax.experimental import pallas as pl
from jax.experimental.pallas import tpu as pltpu
from jax.sharding import Mesh
from jax.sharding import PartitionSpec as P

HD = 128
ZH, X, Y, C = 2, 4, 8, 2
XQ, YQ = X // 2, Y // 2
RG, CB = 2, 4
AXES = ("zh", "x", "y", "c", "rg", "cb")
DP, MP = AXES[:4], AXES[4:]


def place(zh, x, y, c):
    return ((zh * X + x % X) * Y + y % Y) * C + c


FAR = [
    [place(zh, 2 * xq + px, 2 * yq + py, c) for xq in range(XQ) for yq in range(YQ)]
    for zh in range(ZH) for c in range(C) for px in range(2) for py in range(2)
]
NEAR = [
    [
        (
            place(zh, x, y, c),
            place(
                zh,
                x + dx * (1 - 2 * (x % 2)) * (1 - 2 * c),
                y + dy * (1 - 2 * (y % 2)) * (1 - 2 * c),
                c,
            ),
        )
        for zh in range(ZH) for x in range(X) for y in range(Y) for c in range(C)
    ]
    for dx, dy in ((0, 1), (1, 0), (1, 1))
]
ANYWHERE = pl.BlockSpec(memory_space=pltpu.HBM)


def behind_kernel(*refs):
    pass


def behind(array, after):
    return pl.pallas_call(
        behind_kernel,
        out_shape=jax.ShapeDtypeStruct(array.shape, array.dtype),
        in_specs=[ANYWHERE] * (1 + len(after)),
        out_specs=ANYWHERE,
        input_output_aliases={0: 0},
        name="behind",
    )(array, *after)


def spread(block, groups):
    n = len(groups[0])
    blocks = jnp.broadcast_to(block[None], (n,) + block.shape)
    return lax.all_to_all(blocks, DP, 0, 0, axis_index_groups=groups, tiled=True)


def half_sum(px, even, token_refs, w_refs, held_ref, sems):
    moves = [pltpu.make_async_copy(w_refs[i], held_ref.at[even ^ i], sems.at[i]) for i in range(2)]
    for move in moves:
        move.start()
    for move in moves:
        move.wait()
    span = Y * held_ref.shape[4]
    totals = [None, None]
    for zh in range(ZH):
        for xq in range(XQ):
            weight = jnp.concatenate([held_ref[y % 2, xq, y // 2, zh] for y in range(Y)], axis=0)
            start = pl.multiple_of((zh * X + 2 * xq + px) * span, span)
            for g, ref in enumerate(token_refs):
                product = jnp.dot(ref[:, pl.ds(start, span)], weight, preferred_element_type=jnp.float32)
                totals[g] = product if totals[g] is None else totals[g] + product
    return totals


def half_kernel(place_ref, own_ref, other_ref, w0_ref, w1_ref, out_ref, held_ref, sems):
    me = place_ref[0]
    totals = half_sum(me // 2, me % 2, (own_ref, other_ref), (w0_ref, w1_ref), held_ref, sems)
    for g in range(2):
        out_ref[g] = totals[g]


def attend_kernel(place_ref, own_ref, other_ref, half_ref, w0_ref, w1_ref, after_ref, out_ref, held_ref, sems):
    me, core = place_ref[0], place_ref[1]
    totals = half_sum(1 - me // 2, me % 2, (own_ref, other_ref), (w0_ref, w1_ref), held_ref, sems)
    totals = [totals[g] + half_ref[g] for g in range(2)]
    for g in range(2):
        projected = totals[g].astype(jnp.bfloat16)
        queries, key_rows, values = (projected[:, i * HD : (i + 1) * HD] for i in range(3))
        scores = lax.dot_general(
            queries, key_rows, (((1,), (1,)), ((), ())), preferred_element_type=jnp.float32
        ) * (1.0 / math.sqrt(HD))
        raised = jnp.exp(scores - jnp.max(scores, axis=-1, keepdims=True))
        attn = (raised / jnp.sum(raised, axis=-1, keepdims=True)).astype(jnp.bfloat16)
        mixed = jnp.dot(attn, values, preferred_element_type=jnp.float32).astype(jnp.bfloat16)
        for cb in range(CB):
            out_ref[(core ^ g) * CB + cb] = mixed


def split_kernel(place_ref, w_ref, after_ref, own_ref, *out_refs):
    column, core = place_ref[0], place_ref[1]
    part, width = out_refs[0].shape
    own_ref[...] = w_ref[:, pl.ds(pl.multiple_of(column * width, width), width)]
    rows = pl.ds(pl.multiple_of(core * part, part), part)
    for i, out_ref in enumerate(out_refs):
        start = pl.multiple_of((column ^ (i + 1)) * width, width)
        out_ref[...] = w_ref[rows, pl.ds(start, width)]


def project_kernel(place_ref, mixed_ref, own_ref, held_ref, partner_ref, out_ref):
    column, core = place_ref[0], place_ref[1]
    mixed = jnp.concatenate([mixed_ref[c, column] for c in range(C)], axis=1)
    term = jnp.dot(mixed, own_ref[...], preferred_element_type=jnp.float32).astype(jnp.bfloat16)
    total = term.astype(jnp.float32)
    for i in range(CB - 1):
        block = column ^ (i + 1)
        mixed = jnp.concatenate([mixed_ref[core, block], mixed_ref[1 - core, block]], axis=1)
        weight = jnp.concatenate([held_ref[i], partner_ref[i]], axis=0)
        term = jnp.dot(mixed, weight, preferred_element_type=jnp.float32).astype(jnp.bfloat16)
        total += term.astype(jnp.float32)
    out_ref[...] = total.astype(out_ref.dtype)


def body(tokens, qkv_weight, out_weight):
    rows, width = tokens.shape
    k_rows = qkv_weight.shape[0]
    other = lax.ppermute(tokens, "c", [(0, 1), (1, 0)])

    heads = qkv_weight.reshape(k_rows, 3, C, HD).transpose(2, 0, 1, 3).reshape(C, k_rows, 3 * HD)
    heads = jnp.broadcast_to(heads[None], (ZH,) + heads.shape).reshape(ZH * C, k_rows, 3 * HD)
    heads = lax.all_to_all(heads, ("zh", "c"), 0, 0, tiled=True)
    first = heads
    heads = spread(heads, FAR)

    column, core = lax.axis_index("cb"), lax.axis_index("c")
    depth, columns = out_weight.shape[0], out_weight.shape[1] // CB
    smem, vmem = pl.BlockSpec(memory_space=pltpu.SMEM), pl.BlockSpec(memory_space=pltpu.VMEM)
    own_weight, *sent = pl.pallas_call(
        split_kernel,
        out_shape=[jax.ShapeDtypeStruct((depth, columns), jnp.bfloat16)]
        + [jax.ShapeDtypeStruct((depth // C, columns), jnp.bfloat16)] * (CB - 1),
        in_specs=[smem, vmem, vmem],
        out_specs=[vmem] * CB,
        compiler_params=pltpu.CompilerParams(vmem_limit_bytes=24 << 20),
        cost_estimate=pl.CostEstimate(flops=0, bytes_accessed=4 << 20, transcendentals=0),
        name="split",
    )(jnp.stack([column, core]), out_weight, first)
    held = [lax.ppermute(block, "cb", [(j, j ^ (i + 1)) for j in range(CB)]) for i, block in enumerate(sent)]

    heads = behind(heads, held[:2]).reshape(XQ, YQ, ZH, C * k_rows, 3 * HD)
    squares = [heads] + [lax.ppermute(heads, DP, pairs) for pairs in NEAR]
    parity = lax.axis_index("x") % 2 * 2 + lax.axis_index("y") % 2

    spot = jnp.stack([parity, core])
    scratch = [pltpu.VMEM((2,) + heads.shape, jnp.bfloat16), pltpu.SemaphoreType.DMA((2,))]
    work = pl.CostEstimate(flops=2 * rows * width * 3 * HD, bytes_accessed=6 << 20, transcendentals=0)
    half = pl.pallas_call(
        half_kernel,
        out_shape=jax.ShapeDtypeStruct((2, rows, 3 * HD), jnp.float32),
        in_specs=[smem] + [vmem] * 2 + [ANYWHERE] * 2,
        out_specs=vmem,
        scratch_shapes=scratch,
        compiler_params=pltpu.CompilerParams(vmem_limit_bytes=32 << 20),
        cost_estimate=work,
        name="half",
    )(spot, tokens, other, squares[0], squares[1])
    mixed = pl.pallas_call(
        attend_kernel,
        out_shape=jax.ShapeDtypeStruct((C * CB, rows, HD), jnp.bfloat16),
        in_specs=[smem] + [vmem] * 3 + [ANYWHERE] * 3,
        out_specs=vmem,
        scratch_shapes=scratch,
        compiler_params=pltpu.CompilerParams(vmem_limit_bytes=32 << 20),
        cost_estimate=work,
        name="attend",
    )(spot, tokens, other, half, squares[2], squares[3], held[2])
    held = jnp.stack(held)
    partner = lax.ppermute(held, "c", [(0, 1), (1, 0)])
    mixed = lax.all_to_all(mixed, ("c", "cb"), 0, 0, tiled=True).reshape(C, CB, rows, HD)

    summed = pl.pallas_call(
        project_kernel,
        out_shape=jax.ShapeDtypeStruct((rows, columns), jnp.bfloat16),
        in_specs=[smem] + [vmem] * 4,
        out_specs=vmem,
        compiler_params=pltpu.CompilerParams(vmem_limit_bytes=24 << 20),
        cost_estimate=pl.CostEstimate(flops=2 * rows * CB * C * HD * columns, bytes_accessed=4 << 20, transcendentals=0),
        name="project",
    )(jnp.stack([column, core]), mixed, own_weight, held, partner)
    part = rows // (RG * CB)
    summed = lax.all_to_all(summed.reshape(RG * CB, part, columns), MP, 0, 0, tiled=True)
    summed = summed.reshape(RG, CB, part, columns).astype(jnp.float32)
    summed = (summed[0] + summed[1]).astype(jnp.bfloat16)
    return summed.transpose(1, 0, 2).reshape(part, CB * columns)


def solution(mesh):
    named = Mesh(mesh.devices.reshape(ZH, X, Y, C, RG, CB), AXES)
    return jax.shard_map(
        body,
        mesh=named,
        in_specs=(P(DP, None), P(DP, None, MP), P(MP, None)),
        out_specs=P(DP + MP, None),
        check_vma=False,
    )
```

```python
import math

import jax
import jax.numpy as jnp
from jax import lax
from jax.experimental import pallas as pl
from jax.experimental.pallas import tpu as pltpu
from jax.sharding import Mesh
from jax.sharding import PartitionSpec as P

HD = 128
ZH, X, Y, C = 2, 4, 8, 2
XQ, YQ = X // 2, Y // 2
RG, CB = 2, 4
AXES = ("zh", "x", "y", "c", "rg", "cb")
DP, MP = AXES[:4], AXES[4:]


def place(zh, x, y, c):
    return ((zh * X + x % X) * Y + y % Y) * C + c


FAR = [
    [place(zh, 2 * xq + px, 2 * yq + py, c) for xq in range(XQ) for yq in range(YQ)]
    for zh in range(ZH) for c in range(C) for px in range(2) for py in range(2)
]
NEAR = [
    [
        (
            place(zh, x, y, c),
            place(
                zh,
                x + dx * (1 - 2 * (x % 2)) * (1 - 2 * c),
                y + dy * (1 - 2 * (y % 2)) * (1 - 2 * c),
                c,
            ),
        )
        for zh in range(ZH) for x in range(X) for y in range(Y) for c in range(C)
    ]
    for dx, dy in ((0, 1), (1, 0), (1, 1))
]
ANYWHERE = pl.BlockSpec(memory_space=pltpu.HBM)


def behind_kernel(*refs):
    pass


def behind(array, after):
    return pl.pallas_call(
        behind_kernel,
        out_shape=jax.ShapeDtypeStruct(array.shape, array.dtype),
        in_specs=[ANYWHERE] * (1 + len(after)),
        out_specs=ANYWHERE,
        input_output_aliases={0: 0},
        name="behind",
    )(array, *after)


def spread(block, groups):
    n = len(groups[0])
    blocks = jnp.broadcast_to(block[None], (n,) + block.shape)
    return lax.all_to_all(blocks, DP, 0, 0, axis_index_groups=groups, tiled=True)


def half_sum(px, even, token_refs, w_refs, held_ref, sems):
    moves = [pltpu.make_async_copy(w_refs[i], held_ref.at[even ^ i], sems.at[i]) for i in range(2)]
    for move in moves:
        move.start()
    for move in moves:
        move.wait()
    span = Y * held_ref.shape[4]
    totals = [None, None]
    for zh in range(ZH):
        for xq in range(XQ):
            weight = jnp.concatenate([held_ref[y % 2, xq, y // 2, zh] for y in range(Y)], axis=0)
            start = pl.multiple_of((zh * X + 2 * xq + px) * span, span)
            for g, ref in enumerate(token_refs):
                product = jnp.dot(ref[:, pl.ds(start, span)], weight, preferred_element_type=jnp.float32)
                totals[g] = product if totals[g] is None else totals[g] + product
    return totals


def half_kernel(place_ref, own_ref, other_ref, w0_ref, w1_ref, out_ref, held_ref, sems):
    me = place_ref[0]
    totals = half_sum(me // 2, me % 2, (own_ref, other_ref), (w0_ref, w1_ref), held_ref, sems)
    for g in range(2):
        out_ref[g] = totals[g]


def attend_kernel(place_ref, own_ref, other_ref, half_ref, w0_ref, w1_ref, after_ref, out_ref, held_ref, sems):
    me, core = place_ref[0], place_ref[1]
    totals = half_sum(1 - me // 2, me % 2, (own_ref, other_ref), (w0_ref, w1_ref), held_ref, sems)
    totals = [totals[g] + half_ref[g] for g in range(2)]
    for g in range(2):
        projected = totals[g].astype(jnp.bfloat16)
        queries, key_rows, values = (projected[:, i * HD : (i + 1) * HD] for i in range(3))
        scores = lax.dot_general(
            queries, key_rows, (((1,), (1,)), ((), ())), preferred_element_type=jnp.float32
        ) * (1.0 / math.sqrt(HD))
        raised = jnp.exp(scores - jnp.max(scores, axis=-1, keepdims=True))
        attn = (raised / jnp.sum(raised, axis=-1, keepdims=True)).astype(jnp.bfloat16)
        mixed = jnp.dot(attn, values, preferred_element_type=jnp.float32).astype(jnp.bfloat16)
        for cb in range(CB):
            out_ref[(core ^ g) * CB + cb] = mixed


def split_kernel(place_ref, w_ref, *refs):
    column, core = place_ref[0], place_ref[1]
    out_refs = refs[1:]
    part, width = out_refs[0].shape
    rows = pl.ds(pl.multiple_of(core * part, part), part)
    for i, out_ref in enumerate(out_refs):
        start = pl.multiple_of((column ^ (i + 1)) * width, width)
        out_ref[...] = w_ref[rows, pl.ds(start, width)]


def project_kernel(place_ref, mixed_ref, w_ref, held_ref, partner_ref, out_ref, own_ref, sem):
    column, core = place_ref[0], place_ref[1]
    width = own_ref.shape[1]
    fetch = pltpu.make_async_copy(
        w_ref.at[:, pl.ds(pl.multiple_of(column * width, width), width)], own_ref, sem
    )
    fetch.start()
    total = None
    for i in range(CB - 1):
        block = column ^ (i + 1)
        mixed = jnp.concatenate([mixed_ref[core, block], mixed_ref[1 - core, block]], axis=1)
        weight = jnp.concatenate([held_ref[i], partner_ref[i]], axis=0)
        term = jnp.dot(mixed, weight, preferred_element_type=jnp.float32).astype(jnp.bfloat16)
        wide = term.astype(jnp.float32)
        total = wide if total is None else total + wide
    fetch.wait()
    mixed = jnp.concatenate([mixed_ref[c, column] for c in range(C)], axis=1)
    term = jnp.dot(mixed, own_ref[...], preferred_element_type=jnp.float32).astype(jnp.bfloat16)
    out_ref[...] = (total + term.astype(jnp.float32)).astype(out_ref.dtype)


def body(tokens, qkv_weight, out_weight):
    rows, width = tokens.shape
    k_rows = qkv_weight.shape[0]
    other = lax.ppermute(tokens, "c", [(0, 1), (1, 0)])

    heads = qkv_weight.reshape(k_rows, 3, C, HD).transpose(2, 0, 1, 3).reshape(C, k_rows, 3 * HD)
    heads = jnp.broadcast_to(heads[None], (ZH,) + heads.shape).reshape(ZH * C, k_rows, 3 * HD)
    heads = lax.all_to_all(heads, ("zh", "c"), 0, 0, tiled=True)
    first = heads
    heads = spread(heads, FAR)

    column, core = lax.axis_index("cb"), lax.axis_index("c")
    depth, columns = out_weight.shape[0], out_weight.shape[1] // CB
    smem, vmem = pl.BlockSpec(memory_space=pltpu.SMEM), pl.BlockSpec(memory_space=pltpu.VMEM)
    sent = pl.pallas_call(
        split_kernel,
        out_shape=[jax.ShapeDtypeStruct((depth // C, columns), jnp.bfloat16)] * (CB - 1),
        in_specs=[smem, vmem, vmem],
        out_specs=[vmem] * (CB - 1),
        compiler_params=pltpu.CompilerParams(vmem_limit_bytes=24 << 20),
        cost_estimate=pl.CostEstimate(flops=0, bytes_accessed=4 << 20, transcendentals=0),
        name="split",
    )(jnp.stack([column, core]), out_weight, first)
    held = [lax.ppermute(block, "cb", [(j, j ^ (i + 1)) for j in range(CB)]) for i, block in enumerate(sent)]

    heads = behind(heads, held[:2]).reshape(XQ, YQ, ZH, C * k_rows, 3 * HD)
    squares = [heads] + [lax.ppermute(heads, DP, pairs) for pairs in NEAR]
    parity = lax.axis_index("x") % 2 * 2 + lax.axis_index("y") % 2

    spot = jnp.stack([parity, core])
    scratch = [pltpu.VMEM((2,) + heads.shape, jnp.bfloat16), pltpu.SemaphoreType.DMA((2,))]
    work = pl.CostEstimate(flops=2 * rows * width * 3 * HD, bytes_accessed=6 << 20, transcendentals=0)
    half = pl.pallas_call(
        half_kernel,
        out_shape=jax.ShapeDtypeStruct((2, rows, 3 * HD), jnp.float32),
        in_specs=[smem] + [vmem] * 2 + [ANYWHERE] * 2,
        out_specs=vmem,
        scratch_shapes=scratch,
        compiler_params=pltpu.CompilerParams(vmem_limit_bytes=32 << 20),
        cost_estimate=work,
        name="half",
    )(spot, tokens, other, squares[0], squares[1])
    mixed = pl.pallas_call(
        attend_kernel,
        out_shape=jax.ShapeDtypeStruct((C * CB, rows, HD), jnp.bfloat16),
        in_specs=[smem] + [vmem] * 3 + [ANYWHERE] * 3,
        out_specs=vmem,
        scratch_shapes=scratch,
        compiler_params=pltpu.CompilerParams(vmem_limit_bytes=32 << 20),
        cost_estimate=work,
        name="attend",
    )(spot, tokens, other, half, squares[2], squares[3], held[2])
    held = jnp.stack(held)
    partner = lax.ppermute(held, "c", [(0, 1), (1, 0)])
    mixed = lax.all_to_all(mixed, ("c", "cb"), 0, 0, tiled=True).reshape(C, CB, rows, HD)

    summed = pl.pallas_call(
        project_kernel,
        out_shape=jax.ShapeDtypeStruct((rows, columns), jnp.bfloat16),
        in_specs=[smem, vmem, ANYWHERE, vmem, vmem],
        out_specs=vmem,
        scratch_shapes=[pltpu.VMEM((depth, columns), jnp.bfloat16), pltpu.SemaphoreType.DMA(())],
        compiler_params=pltpu.CompilerParams(vmem_limit_bytes=24 << 20),
        cost_estimate=pl.CostEstimate(flops=2 * rows * CB * C * HD * columns, bytes_accessed=4 << 20, transcendentals=0),
        name="project",
    )(jnp.stack([column, core]), mixed, out_weight, held, partner)
    part = rows // (RG * CB)
    summed = lax.all_to_all(summed.reshape(RG * CB, part, columns), MP, 0, 0, tiled=True)
    summed = summed.reshape(RG, CB, part, columns).astype(jnp.float32)
    summed = (summed[0] + summed[1]).astype(jnp.bfloat16)
    return summed.transpose(1, 0, 2).reshape(part, CB * columns)


def solution(mesh):
    named = Mesh(mesh.devices.reshape(ZH, X, Y, C, RG, CB), AXES)
    return jax.shard_map(
        body,
        mesh=named,
        in_specs=(P(DP, None), P(DP, None, MP), P(MP, None)),
        out_specs=P(DP + MP, None),
        check_vma=False,
    )
```
